32 devices in a mesh: gx: 2 (over core), gy: 16 (over z, y, x).
Axes of the slice: x: 2, y: 2, z: 4, core: 2. Of those that a mesh axis runs over, the one named last changes fastest.
Arguments:
- velocity: float32 [2, 32, 256, 2048], P(None, None, 'gx', 'gy'), may hold values from -2.5 to 2.5
- stream_metric: float32 [256], replicated, may hold values from 0.5 to 2
- wall_metric: float32 [2048], replicated, may hold values from 0.5 to 2
Outputs:
- advection: float32 [3, 32, 256, 2048], P(None, None, 'gx', 'gy')
The draws below stay inside these ranges and needn't reach their ends.
All inputs are finite; a program needn't handle non-finite values.
Results may differ from the reference program's by a relative error of at most 0.0003.
Values sent between devices are 32-bit elements; how exact they have to be, the bound alone decides.
No kernel may reach another device: no remote copies, remote signals or barrier semaphores. Data moves between devices by JAX's collectives and lax.ppermute only.
A program may use at most 256 MiB of HBM per device.

```python
import math
import jax
import jax.numpy as jnp
from jax import lax

NZ = 32
NX = 256
NY = 2048


def steps_of(rng, shape, shards, least, high):
    loudness, own = 1.0, jax.random.fold_in(rng, 6)
    for position, shards_of in shards:
        draws = jnp.exp(jax.random.uniform(jax.random.fold_in(own, position), (shards_of,), jnp.float32, least / len(shards), high / len(shards)))
        loudness = loudness * jnp.repeat(draws, shape[position] // shards_of).reshape([-1 if axis == position else 1 for axis in range(len(shape))])
    return loudness


def normal_values(rng, shape, spread, most, cuts=(), kind=jnp.bfloat16):
    factor_of = steps_of(rng, shape, cuts, -0.22, 0.18) if cuts else 1.0
    values = jax.random.normal(rng, shape, jnp.float32) * spread * factor_of
    return jnp.minimum(jnp.maximum(values, -most), most).astype(kind)


def setup_inputs(seed: int = 0) -> dict:
    keys = jax.random.split(jax.random.key(seed), 4)
    return {
        "velocity": normal_values(keys[0], (2, NZ, NX, NY), 0.25, 2.5, ((2, 2), (3, 16)), jnp.float32),
        "stream_metric": jnp.clip(jnp.exp(jax.random.uniform(keys[1], (NX,), jnp.float32, math.log(0.5), math.log(2.0))), 0.5, 2.0),
        "wall_metric": jnp.clip(jnp.exp(jax.random.uniform(keys[2], (NY,), jnp.float32, math.log(0.5), math.log(2.0))), 0.5, 2.0),
    }


CENTRAL = (0.75, -0.15, 1.0 / 60.0)


def periodic_slope(values, dimension):
    result = jnp.zeros_like(values)
    for distance, weight in enumerate(CENTRAL, start=1):
        result = result + weight * (jnp.roll(values, -distance, axis=dimension) - jnp.roll(values, distance, axis=dimension))
    return result


def wall_slope(values):
    rows_all = values.shape[-1]
    pad_width = [(0, 0)] * (values.ndim - 1) + [(3, 3)]
    padded = jnp.pad(values, pad_width)

    def shifted(offset):
        return padded[..., 3 + offset:3 + offset + rows_all]

    result = jnp.zeros_like(values)
    for distance, weight in enumerate(CENTRAL, start=1):
        result = result + weight * (shifted(distance) - shifted(-distance))
    first_row = (-11.0 * values[..., 0] + 18.0 * values[..., 1] - 9.0 * values[..., 2] + 2.0 * values[..., 3]) / 6.0
    second_row = (-2.0 * values[..., 0] - 3.0 * values[..., 1] + 6.0 * values[..., 2] - values[..., 3]) / 6.0
    third_row = (8.0 * (values[..., 3] - values[..., 1]) - (values[..., 4] - values[..., 0])) / 12.0
    third_last = (8.0 * (values[..., -2] - values[..., -4]) - (values[..., -1] - values[..., -5])) / 12.0
    second_last = (2.0 * values[..., -1] + 3.0 * values[..., -2] - 6.0 * values[..., -3] + values[..., -4]) / 6.0
    last_row = (11.0 * values[..., -1] - 18.0 * values[..., -2] + 9.0 * values[..., -3] - 2.0 * values[..., -4]) / 6.0
    result = result.at[..., 0].set(first_row)
    result = result.at[..., 1].set(second_row)
    result = result.at[..., 2].set(third_row)
    result = result.at[..., -3].set(third_last)
    result = result.at[..., -2].set(second_last)
    result = result.at[..., -1].set(last_row)
    return result


def reference(velocity, stream_metric, wall_metric):
    streamwise = velocity[0]
    spanwise = velocity[1]
    stream_scale = stream_metric[None, :, None]
    wall_scale = wall_metric[None, None, :]
    divergence = stream_scale * periodic_slope(streamwise, 1) + periodic_slope(spanwise, 0)
    slope = divergence / wall_scale
    cell_height = 1.0 / wall_metric
    height = jnp.cumsum(cell_height) - 0.5 * cell_height
    total_height = jnp.sum(cell_height)
    rise = jnp.cumsum(slope, axis=2) - 0.5 * slope
    rise_total = jnp.sum(slope, axis=2)
    normal = -(rise - (height / total_height)[None, None, :] * rise_total[:, :, None])
    fields = jnp.stack([streamwise, normal, spanwise])
    offsets = jnp.arange(-3, 4, dtype=jnp.int32)
    stream_plane = stream_metric[None, :, None]
    wall_plane = wall_metric[None, None, :]

    def one_plane(plane_index, output):
        indices = (plane_index + offsets).astype(jnp.int32) % NZ
        planes = jnp.take(fields, indices, axis=1)
        span_products = planes[2:3] * planes
        span_slopes = jnp.zeros_like(planes[:, 3])
        span_fluxes = jnp.zeros_like(planes[:, 3])
        for distance, weight in enumerate(CENTRAL, start=1):
            span_slopes = span_slopes + weight * (planes[:, 3 + distance] - planes[:, 3 - distance])
            span_fluxes = span_fluxes + weight * (span_products[:, 3 + distance] - span_products[:, 3 - distance])
        middle = planes[:, 3]
        stream_slopes = periodic_slope(middle, 1) * stream_plane
        stream_fluxes = periodic_slope(middle[0:1] * middle, 1) * stream_plane
        wall_slopes = wall_slope(middle) * wall_plane
        wall_fluxes = wall_slope(middle[1:2] * middle) * wall_plane
        advection = 0.5 * (middle[0] * stream_slopes + middle[1] * wall_slopes + middle[2] * span_slopes + stream_fluxes + wall_fluxes + span_fluxes)
        return lax.dynamic_update_index_in_dim(output, advection, plane_index, axis=1)

    initial = jnp.zeros((3,) + velocity.shape[1:], jnp.float32)
    return lax.fori_loop(0, NZ, one_plane, initial)
```

```python
import jax
import jax.numpy as jnp
from jax import lax
from jax.experimental import pallas as pl
from jax.experimental.pallas import tpu as pltpu
from jax.sharding import PartitionSpec as P

F32 = jnp.float32
BF16 = jnp.bfloat16
HALF60 = 0.5 / 60.0
CENTRAL = ((1, 45.0), (2, -9.0), (3, 1.0))
WALL_ROWS = (
    {0: -110.0, 1: 180.0, 2: -90.0, 3: 20.0},
    {-1: -20.0, 0: -30.0, 1: 60.0, 2: -10.0},
    {-2: 5.0, -1: -40.0, 1: 40.0, 2: -5.0},
)
LANES = 128
EDGE = 8
LOW = EDGE - 3

WHOLE = pl.BlockSpec(memory_space=pltpu.VMEM)
ANY = pl.BlockSpec(memory_space=pl.ANY)


def iota(shape, dim):
    return lax.broadcasted_iota(jnp.int32, shape, dim)


def split(value):
    high = value.astype(BF16)
    low = (value - high.astype(F32)).astype(BF16)
    return jnp.concatenate([high, low], axis=1)


def wrapped(plane, nz):
    return lax.rem(plane + nz, nz)


def wall_matrix(place, last):
    h = iota((LANES, LANES), 0)
    j = iota((LANES, LANES), 1)
    away = h - j
    inner = jnp.zeros((LANES, LANES), F32)
    for distance, weight in CENTRAL:
        inner = jnp.where(away == distance, weight, inner)
        inner = jnp.where(away == -distance, -weight, inner)
    for row, entries in enumerate(WALL_ROWS):
        for side in (0, 1):
            at = row if side == 0 else LANES - 1 - row
            sign = 1 if side == 0 else -1
            closed = jnp.zeros((LANES, LANES), F32)
            for offset, weight in entries.items():
                closed = jnp.where(away == sign * offset, sign * weight, closed)
            here = jnp.where(place == (0 if side == 0 else last), 1, 0)
            inner = jnp.where((j == at) & (here == 1), closed, inner)
    inner = inner.astype(BF16)
    return jnp.concatenate([inner, inner], axis=0)


def prepare(nz, vel, xr, metric, wall, pad, v0, strip_a, strip_b, sums, mh, ms, slope_s, turned, sems):
    gx = lax.axis_index("gx")
    gy = lax.axis_index("gy")
    columns = metric.shape[1]
    chunks = 8
    per = nz // chunks

    def chunk(c):
        planes = pl.ds(c * per, per)
        return pltpu.make_async_copy(vel.at[:, planes], pad.at[:, planes, pl.ds(EDGE, columns)], sems.at[c])

    for c in range(chunks):
        chunk(c).start()
    right = pltpu.make_async_copy(xr.at[:, :, pl.ds(0, EDGE)], pad.at[:, :, pl.ds(EDGE + columns, EDGE)], sems.at[chunks])
    left = pltpu.make_async_copy(xr.at[:, :, pl.ds(EDGE, EDGE)], pad.at[:, :, pl.ds(0, EDGE)], sems.at[chunks + 1])
    right.start()
    left.start()

    own = jnp.broadcast_to(metric[pl.ds(gx, 1), :], (LANES, columns)).T
    peer = jnp.broadcast_to(metric[pl.ds(1 - gx, 1), :], (LANES, columns)).T
    ms[0:EDGE, :] = peer[columns - EDGE :]
    ms[EDGE : EDGE + columns, :] = own
    ms[EDGE + columns :, :] = peer[:EDGE]
    mh[...] = ms[...] * HALF60
    rw60 = 1.0 / (60.0 * wall[pl.ds(gy, 1), :])
    h = iota((LANES, LANES), 0)
    j = iota((LANES, LANES), 1)
    climb = jnp.where(h < j, -1.0, jnp.where(h == j, -0.5, 0.0)).astype(BF16)
    climb = jnp.concatenate([climb, jnp.ones((LANES, LANES), BF16)], axis=1)
    climb = jnp.concatenate([climb, climb], axis=0)
    rows = columns + EDGE
    lane = iota((rows, LANES), 1)
    lane_c = iota((columns, LANES), 1)
    odd = lax.rem(gy, 2) == 1
    sums[...] = jnp.zeros((rows, LANES), F32)
    right.wait()
    left.wait()
    chunk(0).wait()
    chunk(1).wait()

    def plane(step, _):
        z = lax.rem(step, nz)
        ups = [wrapped(z + d, nz) for d in (1, 2, 3)]
        downs = [wrapped(z - d, nz) for d in (1, 2, 3)]
        blocks = []
        for k in range(rows // 8):
            r = LOW + 8 * k
            du = dw = None
            for distance, weight in CENTRAL:
                a = pad[0, z, pl.ds(r + distance, 8), :] - pad[0, z, pl.ds(r - distance, 8), :]
                b = pad[1, ups[distance - 1], pl.ds(r, 8), :] - pad[1, downs[distance - 1], pl.ds(r, 8), :]
                if weight != 1.0:
                    a, b = weight * a, weight * b
                du = a if du is None else du + a
                dw = b if dw is None else dw + b
            slope = (ms[pl.ds(r, 8), :] * du + dw) * rw60
            slope_s[pl.ds(8 * k, 8), :] = slope
            blocks.append(slope)
        result = jnp.dot(split(jnp.concatenate(blocks, axis=0)), climb, preferred_element_type=F32)
        v0[z, pl.ds(LOW, rows), :] = result[:, :LANES]
        sums[...] = jnp.where(lane == z, result[:, LANES:], sums[...])
        packed = jnp.where(
            lane_c < 6,
            pltpu.roll(pad[0, z, pl.ds(EDGE, columns), :], 3, 1),
            jnp.where(
                lane_c < 12,
                pltpu.roll(pad[1, z, pl.ds(EDGE, columns), :], 9, 1),
                pltpu.roll(slope_s[pl.ds(3, columns), :], 15, 1),
            ),
        )
        turned[...] = packed.T[:24]
        for f in range(3):
            last = turned[6 * f : 6 * f + 3, :]
            first = turned[6 * f + 3 : 6 * f + 6, :]
            strip_a[pl.ds(3 * f * nz + z, 3, stride=nz), :] = jnp.where(odd, first, last)
            strip_b[pl.ds(3 * f * nz + z, 3, stride=nz), :] = jnp.where(odd, last, first)
        return 0

    def group(g, _):
        @pl.when(g < chunks - 2)
        def _():
            chunk(g + 2).wait()

        return lax.fori_loop(per * g + 3, per * g + 3 + per, plane, 0)

    lax.fori_loop(0, chunks, group, 0)


def stream_terms(nz, pad, mh, part, gx_out):
    columns = part.shape[2]

    def plane(z, _):
        for k in range(-1, columns // 8):
            r = EDGE + 8 * k
            u = pad[0, z, pl.ds(r, 8), :]
            total = [None, None]
            for distance, weight in CENTRAL:
                g = u + pad[0, z, pl.ds(r + distance, 8), :]
                if weight != 1.0:
                    g = weight * g
                gx_out[distance - 1, z, pl.ds(r, 8), :] = g
                if k < 0:
                    continue
                g_low = gx_out[distance - 1, z, pl.ds(r - distance, 8), :]
                for c in range(2):
                    term = g * pad[c, z, pl.ds(r + distance, 8), :] - g_low * pad[c, z, pl.ds(r - distance, 8), :]
                    total[c] = term if total[c] is None else total[c] + term
            if k >= 0:
                for c in range(2):
                    part[c, z, pl.ds(8 * k, 8), :] = total[c] * mh[pl.ds(r, 8), :]
        return 0

    lax.fori_loop(0, nz, plane, 0)


def span_terms(nz, pad, part, out, gz_out):
    columns = part.shape[2]

    def factors(z, k):
        r = EDGE + 8 * k
        w = pad[1, z, pl.ds(r, 8), :]
        made = []
        for distance, weight in CENTRAL:
            g = (w + pad[1, wrapped(z + distance, nz), pl.ds(r, 8), :]) * (weight * HALF60)
            gz_out[distance - 1, z, pl.ds(8 * k, 8), :] = g
            made.append(g)
        return made

    def first(z, _):
        for k in range(columns // 8):
            factors(z, k)
        return 0

    def plane(z, _):
        for k in range(columns // 8):
            r = EDGE + 8 * k
            made = factors(z, k)
            total = [part[c, z, pl.ds(8 * k, 8), :] for c in range(2)]
            for distance, _w in CENTRAL:
                up, down = wrapped(z + distance, nz), wrapped(z - distance, nz)
                g_low = gz_out[distance - 1, down, pl.ds(8 * k, 8), :]
                for c in range(2):
                    total[c] = total[c] + (made[distance - 1] * pad[c, up, pl.ds(r, 8), :] - g_low * pad[c, down, pl.ds(r, 8), :])
            for c in range(2):
                out[c, z, pl.ds(8 * k, 8), :] = total[c]
        return 0

    lax.fori_loop(nz - 3, nz, first, 0)
    lax.fori_loop(0, nz, plane, 0)


def wall_terms(nz, last, pad, wall, out):
    gy = lax.axis_index("gy")
    columns = out.shape[2]
    matrix = wall_matrix(gy, last)
    scale = wall[pl.ds(gy, 1), :] * HALF60

    def plane(z, _):
        for c in range(2):
            value = pad[c, z, pl.ds(EDGE, columns), :]
            out[c, z] = jnp.dot(split(value), matrix, preferred_element_type=F32) * scale
        return 0

    lax.fori_loop(0, nz, plane, 0)


def heights(wall, block, blocks):
    cell = 1.0 / wall[...]
    row = iota(cell.shape, 0)
    total = jnp.sum(cell)
    before = jnp.sum(jnp.where(row < block, cell, 0.0))
    mine = 1.0 / wall[pl.ds(block, 1), :]
    prefix = mine
    lane = iota((1, LANES), 1)
    for shift in (1, 2, 4, 8, 16, 32, 64):
        prefix = prefix + jnp.where(lane >= shift, pltpu.roll(prefix, shift, 1), 0.0)
    return (before + prefix - 0.5 * mine) / total


def finish(nz, last, pad, v0, part, dwall, gxs, gzs, mh, wall, own_a, own_b, got_a, got_b, below, total, sums, out, v, buf, fixes, lhs, sems):
    gy = lax.axis_index("gy")
    columns = buf.shape[2]
    rows = columns + EDGE
    odd = lax.rem(gy, 2) == 1
    matrix = wall_matrix(gy, last)
    scale = wall[pl.ds(gy, 1), :] * HALF60
    frac = heights(wall, gy, last + 1)
    frac_low = heights(wall, jnp.maximum(gy - 1, 0), last + 1)
    frac_high = heights(wall, jnp.minimum(gy + 1, last), last + 1)

    def strip(pick, f, r):
        at = pl.ds((3 * f + r) * nz, nz)
        return pick[0][at, :], pick[1][at, :]

    def own_first(f, r):
        a, b = strip((own_a, own_b), f, r)
        return jnp.where(odd, a, b)

    def own_last(f, r):
        a, b = strip((own_a, own_b), f, r)
        return jnp.where(odd, b, a)

    def from_low(f, r):
        a, b = strip((got_a, got_b), f, r)
        return jnp.where(odd, a, b)

    def from_high(f, r):
        a, b = strip((got_a, got_b), f, r)
        return jnp.where(odd, b, a)

    def compact(ref):
        return ref[pl.ds(3, columns), :].T[:nz]

    below_c = compact(below)
    total_c = compact(total)
    incl_c = below_c + compact(sums)
    lane_one = lambda vector, at: vector[:, at : at + 1]

    def climb(start, slopes, sign, fractions):
        level, made = start, []
        for slope, fraction in zip(slopes, fractions):
            made.append(fraction * total_c - (level + (0.5 * sign) * slope))
            level = level + sign * slope
        return made

    v_first = climb(below_c, [own_first(2, r) for r in range(3)], 1.0, [lane_one(frac, r) for r in range(3)])
    v_last = climb(incl_c, [own_last(2, 2 - q) for q in range(3)], -1.0, [lane_one(frac, LANES - 1 - q) for q in range(3)])
    v_low = climb(below_c, [from_low(2, 2 - q) for q in range(3)], -1.0, [lane_one(frac_low, LANES - 1 - q) for q in range(3)])
    v_high = climb(incl_c, [from_high(2, r) for r in range(3)], 1.0, [lane_one(frac_high, r) for r in range(3)])
    v_low = [jnp.where(gy > 0, x, 0.0) for x in v_low]
    v_high = [jnp.where(gy < last, x, 0.0) for x in v_high]
    weight_of = dict(CENTRAL)
    for i in range(24):
        if i % 8 >= 6:
            fixes[pl.ds(i * nz, nz), :] = jnp.zeros((nz, LANES), F32)
    for c in range(3):
        for side in range(2):
            v_own, v_out = (v_first, v_low) if side == 0 else (v_last, v_high)
            for q in range(3):
                value = None
                for m in range(3 - q):
                    if c == 1:
                        field = v_out[m]
                    elif side == 0:
                        field = from_low(c // 2, 2 - m)
                    else:
                        field = from_high(c // 2, m)
                    weight = weight_of[q + m + 1] * (-1.0 if side == 0 else 1.0)
                    term = weight * ((v_own[q] + v_out[m]) * field)
                    value = term if value is None else value + term
                slot = 3 + q if side == 0 else 2 - q
                at = q if side == 0 else LANES - 1 - q
                fixes[pl.ds((8 * c + slot) * nz, nz), :] = value * lane_one(scale, at)

    below_v = below[...]
    total_v = total[...]
    below_h = below_v.astype(BF16).astype(F32)
    below_l = below_v - below_h
    total_h = total_v.astype(BF16).astype(F32)
    total_l = total_v - total_h
    quarter = iota((rows, LANES), 1) // nz
    first_half = jnp.where(
        quarter == 0,
        below_h,
        jnp.where(
            quarter == 1,
            pltpu.roll(below_l, nz, 1),
            jnp.where(quarter == 2, pltpu.roll(total_h, 2 * nz, 1), pltpu.roll(total_l, 3 * nz, 1)),
        ),
    )
    second_half = jnp.where(quarter == 0, total_h, jnp.where(quarter == 1, pltpu.roll(total_l, nz, 1), 0.0))
    lhs[:, :LANES] = first_half.astype(BF16)
    lhs[:, LANES:] = second_half.astype(BF16)
    frac_h = frac.astype(BF16).astype(F32)
    frac_l = frac - frac_h
    k_index = iota((2 * LANES, LANES), 0)
    base = jnp.where(
        k_index < 2 * nz,
        -1.0,
        jnp.where(k_index < LANES, jnp.broadcast_to(frac_h, (2 * LANES, LANES)), jnp.broadcast_to(frac_l, (2 * LANES, LANES))),
    )
    k_plane = lax.rem(k_index, nz)

    def make_v(step):
        z = wrapped(step, nz)
        chosen = jnp.where(k_plane == z, base, 0.0).astype(BF16)
        v[z, pl.ds(LOW, rows), :] = v0[z, pl.ds(LOW, rows), :] + jnp.dot(lhs[...], chosen, preferred_element_type=F32)

    def make_first(step, _):
        make_v(step)
        return 0

    lax.fori_loop(nz - 3, nz + 4, make_first, 0)
    lane = iota((columns, LANES), 1)
    at_edge = (lane < 3) | (lane >= LANES - 3)
    zeros = jnp.zeros((LANES - 24, LANES), F32)
    chunks = 8
    per = nz // chunks

    def plane(z, _):
        @pl.when(z < nz - 7)
        def _():
            make_v(z + 4)

        turned = jnp.concatenate([fixes[pl.ds(z, 24, stride=nz), :], zeros], axis=0).T
        fix = [jnp.where(at_edge, pltpu.roll(turned, LANES - 3 - 8 * c, 1), 0.0) for c in range(3)]
        here = v[z, pl.ds(EDGE, columns), :]
        d_v = jnp.dot(split(here), matrix, preferred_element_type=F32)
        d_vv = jnp.dot(split(here * here), matrix, preferred_element_type=F32)
        d_vu = jnp.dot(split(here * pad[0, z, pl.ds(EDGE, columns), :]), matrix, preferred_element_type=F32)
        d_vw = jnp.dot(split(here * pad[1, z, pl.ds(EDGE, columns), :]), matrix, preferred_element_type=F32)
        buf[0, z] = part[0, z] + here * dwall[0, z] + (scale * d_vu + fix[0])
        buf[2, z] = part[1, z] + here * dwall[1, z] + (scale * d_vw + fix[2])
        for k in range(columns // 8):
            r = EDGE + 8 * k
            at = pl.ds(8 * k, 8)
            across = along = None
            for distance, _w in CENTRAL:
                up, down = wrapped(z + distance, nz), wrapped(z - distance, nz)
                a = gxs[distance - 1, z, pl.ds(r, 8), :] * v[z, pl.ds(r + distance, 8), :]
                a = a - gxs[distance - 1, z, pl.ds(r - distance, 8), :] * v[z, pl.ds(r - distance, 8), :]
                b = gzs[distance - 1, z, at, :] * v[up, pl.ds(r, 8), :]
                b = b - gzs[distance - 1, down, at, :] * v[down, pl.ds(r, 8), :]
                across = a if across is None else across + a
                along = b if along is None else along + b
            rows_k = slice(8 * k, 8 * k + 8)
            wallward = scale * (here[rows_k] * d_v[rows_k] + d_vv[rows_k]) + fix[1][rows_k]
            buf[1, z, at, :] = across * mh[pl.ds(r, 8), :] + along + wallward
        return 0

    def send(c):
        planes = pl.ds(c * per, per)
        return pltpu.make_async_copy(buf.at[:, planes], out.at[:, planes], sems.at[c])

    def group(g, _):
        lax.fori_loop(per * g, per * g + per, plane, 0)
        send(g).start()
        return 0

    lax.fori_loop(0, chunks, group, 0)
    for c in range(chunks):
        send(c).wait()


def call(body, name, inputs, specs, outputs, scratch, flops, moved, limit):
    return pl.pallas_call(
        body,
        name=name,
        in_specs=specs,
        out_specs=tuple(ANY if isinstance(o, jax.ShapeDtypeStruct) else WHOLE for o in outputs),
        out_shape=tuple(outputs),
        scratch_shapes=scratch,
        cost_estimate=pl.CostEstimate(flops=flops, bytes_accessed=moved, transcendentals=0),
        compiler_params=pltpu.CompilerParams(vmem_limit_bytes=limit),
    )(*inputs)


def keep(value):
    return pltpu.with_memory_space_constraint(value, pltpu.VMEM)


def shards(velocity, stream_metric, wall_metric):
    _, nz, columns, rows_here = velocity.shape
    n_gy = lax.axis_size("gy")
    last = n_gy - 1
    padded = columns + 2 * EDGE
    rows = columns + EDGE
    metric = stream_metric.reshape(2, columns)
    wall = wall_metric.reshape(n_gy, rows_here)

    sent = jnp.concatenate([velocity[:, :, :EDGE], velocity[:, :, columns - EDGE :]], axis=2)
    xr = lax.ppermute(sent, "gx", [(0, 1), (1, 0)])

    volume = nz * columns * rows_here
    mib = 1 << 20
    pad, v0, strip_a, strip_b, sums, mh = call(
        lambda *refs: prepare(nz, *refs),
        "prepare",
        (velocity, xr, metric, wall),
        [ANY, ANY, WHOLE, WHOLE],
        [
            pltpu.VMEM((2, nz, padded, LANES), F32),
            pltpu.VMEM((nz, padded, LANES), F32),
            pltpu.VMEM((9 * nz, LANES), F32),
            pltpu.VMEM((9 * nz, LANES), F32),
            pltpu.VMEM((rows, LANES), F32),
            pltpu.VMEM((padded, LANES), F32),
        ],
        [
            pltpu.VMEM((padded, LANES), F32),
            pltpu.VMEM((rows, LANES), F32),
            pltpu.VMEM((24, LANES), F32),
            pltpu.SemaphoreType.DMA((10,)),
        ],
        30 * volume,
        8 * volume,
        8 * mib,
    )
    pad, v0, mh = keep(pad), keep(v0), keep(mh)

    part, gxs = call(
        lambda *refs: stream_terms(nz, *refs),
        "stream_terms",
        (pad, mh),
        [WHOLE] * 2,
        [pltpu.VMEM((2, nz, columns, LANES), F32), pltpu.VMEM((3, nz, padded, LANES), F32)],
        [],
        40 * volume,
        8 * volume,
        4 * mib,
    )
    part, gxs = keep(part), keep(gxs)
    (dwall,) = call(
        lambda *refs: wall_terms(nz, last, *refs),
        "wall_terms",
        (pad, wall),
        [WHOLE] * 2,
        [pltpu.VMEM((2, nz, columns, LANES), F32)],
        [],
        40 * volume,
        8 * volume,
        4 * mib,
    )
    dwall = keep(dwall)
    part, gzs = call(
        lambda *refs: span_terms(nz, *refs),
        "span_terms",
        (pad, part),
        [WHOLE] * 2,
        [pltpu.VMEM((2, nz, columns, LANES), F32), pltpu.VMEM((3, nz, columns, LANES), F32)],
        [],
        40 * volume,
        8 * volume,
        4 * mib,
    )
    part, gzs = keep(part), keep(gzs)

    place = lax.axis_index("gy")
    pairs = [(i, i ^ 1) for i in range(n_gy)]
    others = [(i, i + 1) if i % 2 else (i, i - 1) for i in range(1, last)]
    total, below = sums, jnp.zeros_like(sums)
    got_a = lax.ppermute(strip_a, "gy", pairs)
    got_b = lax.ppermute(strip_b, "gy", others)
    hop = 1
    while hop < n_gy:
        came = lax.ppermute(total, "gy", [(i, i ^ hop) for i in range(n_gy)])
        below = below + jnp.where((place & hop) != 0, came, 0.0)
        total = total + came
        hop *= 2

    (out,) = call(
        lambda *refs: finish(nz, last, *refs),
        "finish",
        (pad, v0, part, dwall, gxs, gzs, mh, wall, strip_a, strip_b, got_a, got_b, below, total, sums),
        [WHOLE] * 15,
        [jax.ShapeDtypeStruct((3, nz, columns, rows_here), F32)],
        [
            pltpu.VMEM((nz, padded, LANES), F32),
            pltpu.VMEM((3, nz, columns, LANES), F32),
            pltpu.VMEM((24 * nz, LANES), F32),
            pltpu.VMEM((rows, 2 * LANES), BF16),
            pltpu.SemaphoreType.DMA((8,)),
        ],
        80 * volume,
        20 * volume,
        16 * mib,
    )
    return out


def solution(mesh):
    in_specs = (P(None, None, "gx", "gy"), P(), P())
    out_specs = P(None, None, "gx", "gy")
    return jax.shard_map(shards, mesh=mesh, in_specs=in_specs, out_specs=out_specs, check_vma=False)
```

```python
import jax
import jax.numpy as jnp
from jax import lax
from jax.experimental import pallas as pl
from jax.experimental.pallas import tpu as pltpu
from jax.sharding import PartitionSpec as P

F32 = jnp.float32
BF16 = jnp.bfloat16
HALF60 = 0.5 / 60.0
CENTRAL = ((1, 45.0), (2, -9.0), (3, 1.0))
WALL_ROWS = (
    {0: -110.0, 1: 180.0, 2: -90.0, 3: 20.0},
    {-1: -20.0, 0: -30.0, 1: 60.0, 2: -10.0},
    {-2: 5.0, -1: -40.0, 1: 40.0, 2: -5.0},
)
LANES = 128
GROUP = 4
EDGE = 8
LOW = EDGE - 3

WHOLE = pl.BlockSpec(memory_space=pltpu.VMEM)
HBM = pl.BlockSpec(memory_space=pltpu.HBM)


def iota(shape, dim):
    return lax.broadcasted_iota(jnp.int32, shape, dim)


def split(value):
    high = value.astype(BF16)
    low = (value - high.astype(F32)).astype(BF16)
    return jnp.concatenate([high, low], axis=1)


def wrapped(plane, nz):
    return lax.rem(plane + nz, nz)


def wall_matrix(place, last):
    h = iota((LANES, LANES), 0)
    j = iota((LANES, LANES), 1)
    away = h - j
    inner = jnp.zeros((LANES, LANES), F32)
    for distance, weight in CENTRAL:
        inner = jnp.where(away == distance, weight, inner)
        inner = jnp.where(away == -distance, -weight, inner)
    for row, entries in enumerate(WALL_ROWS):
        for side in (0, 1):
            at = row if side == 0 else LANES - 1 - row
            sign = 1 if side == 0 else -1
            closed = jnp.zeros((LANES, LANES), F32)
            for offset, weight in entries.items():
                closed = jnp.where(away == sign * offset, sign * weight, closed)
            here = jnp.where(place == (0 if side == 0 else last), 1, 0)
            inner = jnp.where((j == at) & (here == 1), closed, inner)
    inner = inner.astype(BF16)
    return jnp.concatenate([inner, inner], axis=0)


def heights(wall, block, blocks):
    cell = 1.0 / wall[...]
    row = iota(cell.shape, 0)
    total = jnp.sum(cell)
    before = jnp.sum(jnp.where(row < block, cell, 0.0))
    mine = 1.0 / wall[pl.ds(block, 1), :]
    prefix = mine
    lane = iota((1, LANES), 1)
    for shift in (1, 2, 4, 8, 16, 32, 64):
        prefix = prefix + jnp.where(lane >= shift, pltpu.roll(prefix, shift, 1), 0.0)
    return (before + prefix - 0.5 * mine) / total


def sum_rows(nz, last, vel, metric_hbm, wall_hbm, pad, uw, ms, mh, vectors, matrix, bits, masks, metric, wall, sems):
    gx = lax.axis_index("gx")
    gy = lax.axis_index("gy")
    columns = uw.shape[0]
    chunks = 8
    per = nz // chunks

    def chunk(c):
        planes = pl.ds(c * per, per)
        return pltpu.make_async_copy(vel.at[:, planes], pad.at[:, planes, pl.ds(EDGE, columns)], sems.at[c])

    small = [
        pltpu.make_async_copy(wall_hbm, wall, sems.at[chunks]),
        pltpu.make_async_copy(metric_hbm, metric, sems.at[chunks + 1]),
    ]
    for copy in small:
        copy.start()
    for c in range(chunks):
        chunk(c).start()
    matrix[...] = wall_matrix(gy, last)
    plane = iota(masks.shape, 0) // 8
    masks[...] = jnp.where(lax.rem(iota(masks.shape, 1), nz) == plane, 1.0, 0.0).astype(BF16)
    for copy in small:
        copy.wait()
    own = jnp.broadcast_to(metric[pl.ds(gx, 1), :], (LANES, columns)).T
    peer = jnp.broadcast_to(metric[pl.ds(1 - gx, 1), :], (LANES, columns)).T
    ms[0:EDGE, :] = peer[columns - EDGE :]
    ms[EDGE : EDGE + columns, :] = own
    ms[EDGE + columns :, :] = peer[:EDGE]
    mh[...] = ms[...] * HALF60
    wall_here = wall[pl.ds(gy, 1), :]
    rw = 1.0 / wall_here
    vectors[0:1, :] = heights(wall, jnp.maximum(gy - 1, 0), last + 1)
    vectors[1:2, :] = heights(wall, gy, last + 1)
    vectors[2:3, :] = heights(wall, jnp.minimum(gy + 1, last), last + 1)
    vectors[3:4, :] = wall_here * HALF60
    vectors[4:5, :] = rw
    vectors[5:8, :] = jnp.zeros((3, LANES), F32)
    for i in range(bits.shape[0]):
        bits[i : i + 1, :] = jnp.full((1, LANES), jnp.where((gy & (1 << i)) != 0, 1.0, 0.0), F32)
    lane = iota((columns, LANES), 1)

    def group(g, held):
        chunk(g).wait()
        for p in range(per):
            z = g * per + p
            for c in range(2):
                line = jnp.sum(pad[c, z, pl.ds(EDGE, columns), :] * rw, axis=1, keepdims=True)
                held = jnp.where(lane == z + c * nz, line, held)
        return held

    uw[...] = lax.fori_loop(0, chunks, group, jnp.zeros((columns, LANES), F32))


def sum_slopes(nz, xr, uw, ms, vectors, sums, wide):
    columns = uw.shape[0]
    rows = columns + EDGE
    rw = vectors[4:5, :]
    lane = iota((2 * EDGE, LANES), 1)
    held = jnp.zeros((2 * EDGE, LANES), F32)
    for z in range(nz):
        for c in range(2):
            line = jnp.sum(xr[c, z] * rw, axis=1, keepdims=True)
            held = jnp.where(lane == z + c * nz, line, held)
    wide[0:EDGE, :] = held[EDGE:]
    wide[EDGE : EDGE + columns, :] = uw[...]
    wide[EDGE + columns :, :] = held[:EDGE]
    centre = wide[pl.ds(LOW, rows), :]
    lane = iota((rows, LANES), 1)
    around = jnp.where(lane < nz, pltpu.roll(centre, LANES - nz, 1), centre)
    around = jnp.where(lane < 2 * nz, around, pltpu.roll(around, 2 * nz, 1))
    du = dw = None
    for distance, weight in CENTRAL:
        a = weight * (wide[pl.ds(LOW + distance, rows), :] - wide[pl.ds(LOW - distance, rows), :])
        b = weight * (pltpu.roll(around, LANES - distance, 1) - pltpu.roll(around, distance, 1))
        du = a if du is None else du + a
        dw = b if dw is None else dw + b
    total = (ms[pl.ds(LOW, rows), :] * du + dw) * (1.0 / 60.0)
    sums[...] = jnp.where(lane < nz, total, 0.0)


def edge_columns(first_lane):
    h = iota((LANES, LANES), 0)
    lane = iota((LANES, LANES), 1) - first_lane
    last = (lane >= 0) & (lane < 3) & (h == lane + LANES - 3)
    first = (lane >= 3) & (lane < 6) & (h == lane - 3)
    picked = jnp.where(last | first, 1.0, 0.0).astype(BF16)
    return jnp.concatenate([picked, picked], axis=0)


def prepare(
    nz, pad_in, xr, ms, vectors, matrix, pad, v0, dwall, strip_a, strip_b, token,
    weights_s, weights_u, weights_w, halves_s, halves_u, halves_w, edges, turned,
):
    del pad_in
    gy = lax.axis_index("gy")
    columns = dwall.shape[2]
    rows = columns + EDGE
    tall = rows // 8
    rw60 = vectors[4:5, :] * (1.0 / 60.0)
    scale = vectors[3:4, :]
    h = iota((LANES, LANES), 0)
    j = iota((LANES, LANES), 1)
    climb = jnp.where(h < j, -1.0, jnp.where(h == j, -0.5, 0.0)).astype(BF16)
    weights_s[:, :LANES] = jnp.concatenate([climb, climb], axis=0)
    weights_s[:, LANES:] = edge_columns(12)
    weights_u[:, :LANES] = matrix[...]
    weights_u[:, LANES:] = edge_columns(0)
    weights_w[:, :LANES] = matrix[...]
    weights_w[:, LANES:] = edge_columns(6)
    odd = lax.rem(gy, 2) == 1
    token[...] = jnp.zeros(token.shape, F32)
    pad[:, :, pl.ds(0, EDGE), :] = xr[:, :, pl.ds(EDGE, EDGE), :]
    pad[:, :, pl.ds(EDGE + columns, EDGE), :] = xr[:, :, pl.ds(0, EDGE), :]

    def gather(g):
        blocks = []
        for p in range(GROUP):
            z = g * GROUP + p
            ups = [wrapped(z + d, nz) for d in (1, 2, 3)]
            downs = [wrapped(z - d, nz) for d in (1, 2, 3)]
            for k in range(tall):
                r = LOW + 8 * k
                du = dw = None
                for distance, weight in CENTRAL:
                    a = pad[0, z, pl.ds(r + distance, 8), :] - pad[0, z, pl.ds(r - distance, 8), :]
                    b = pad[1, ups[distance - 1], pl.ds(r, 8), :] - pad[1, downs[distance - 1], pl.ds(r, 8), :]
                    if weight != 1.0:
                        a, b = weight * a, weight * b
                    du = a if du is None else du + a
                    dw = b if dw is None else dw + b
                blocks.append((ms[pl.ds(r, 8), :] * du + dw) * rw60)
                if len(blocks) == 2:
                    halves_s[pl.ds(8 * (p * tall + k - 1), 16), :] = split(jnp.concatenate(blocks, axis=0))
                    blocks = []
            halves_u[pl.ds(p * columns, columns), :] = split(pad[0, z, pl.ds(EDGE, columns), :])
            halves_w[pl.ds(p * columns, columns), :] = split(pad[1, z, pl.ds(EDGE, columns), :])

    def settle(g):
        made_s = jnp.dot(halves_s[...], weights_s[...], preferred_element_type=F32)
        for p in range(GROUP):
            here = made_s[p * rows : (p + 1) * rows]
            v0[g * GROUP + p, pl.ds(LOW, rows), :] = here[:, :LANES]
            edges[p] = here[:, LANES:]
        made_u = jnp.dot(halves_u[...], weights_u[...], preferred_element_type=F32)
        made_w = jnp.dot(halves_w[...], weights_w[...], preferred_element_type=F32)
        for p in range(GROUP):
            z = g * GROUP + p
            at = slice(p * columns, (p + 1) * columns)
            dwall[0, z] = made_u[at, :LANES] * scale
            dwall[1, z] = made_w[at, :LANES] * scale
            packed = made_u[at, LANES:] + made_w[at, LANES:] + edges[p, pl.ds(3, columns), :]
            turned[p] = packed.T[:24]
            for f in range(3):
                last = turned[p, 6 * f : 6 * f + 3, :]
                first = turned[p, 6 * f + 3 : 6 * f + 6, :]
                strip_a[pl.ds(3 * f * nz + z, 3, stride=nz), :] = jnp.where(odd, first, last)
                strip_b[pl.ds(3 * f * nz + z, 3, stride=nz), :] = jnp.where(odd, last, first)

    def step(g, _):
        settle(g)
        gather(g + 1)
        return 0

    groups = nz // GROUP
    gather(0)
    lax.fori_loop(0, groups - 1, step, 0)
    settle(groups - 1)


def known_terms(nz, pad, mh, wait_a, wait_b, pad_out, part, gx_out, gz_out, token):
    del pad_out, wait_a, wait_b
    columns = part.shape[2]
    token[...] = jnp.zeros(token.shape, F32)
    for z in range(nz):
        u = pad[0, z, pl.ds(0, 8), :]
        for distance, weight in CENTRAL:
            gx_out[distance - 1, z, pl.ds(0, 8), :] = weight * (u + pad[0, z, pl.ds(distance, 8), :])

    def block(k, _):
        r = pl.multiple_of(8 * k + EDGE, 8)
        at = pl.ds(pl.multiple_of(8 * k, 8), 8)
        metric = mh[pl.ds(r, 8), :]
        field = [{}, {}]
        factor = {}

        def load(c, z):
            if z not in field[c]:
                field[c][z] = pad[c, z % nz, pl.ds(r, 8), :]
            return field[c][z]

        def span_factor(distance, weight, z):
            if (distance, z) not in factor:
                factor[distance, z] = (load(1, z) + load(1, z + distance)) * (weight * HALF60)
            return factor[distance, z]

        for z in range(nz):
            u = load(0, z)
            across = [None, None]
            along = [None, None]
            for distance, weight in CENTRAL:
                ahead = [pad[c, z, pl.ds(r + distance, 8), :] for c in range(2)]
                behind = [pad[c, z, pl.ds(r - distance, 8), :] for c in range(2)]
                g, g_low = u + ahead[0], u + behind[0]
                if weight != 1.0:
                    g, g_low = weight * g, weight * g_low
                gx_out[distance - 1, z, pl.ds(r, 8), :] = g
                s = span_factor(distance, weight, z)
                s_low = span_factor(distance, weight, z - distance)
                gz_out[distance - 1, z, at, :] = s
                for c in range(2):
                    a = g * ahead[c] - g_low * behind[c]
                    b = s * load(c, z + distance) - s_low * load(c, z - distance)
                    across[c] = a if across[c] is None else across[c] + a
                    along[c] = b if along[c] is None else along[c] + b
            for c in range(2):
                part[c, z, at, :] = across[c] * metric + along[c]
        return 0

    lax.fori_loop(0, columns // 8, block, 0)


def finish(
    nz, last, pad, v0, part, dwall, gxs, gzs, mh, vectors, matrix, masks, own_a, own_b, got_a, got_b, below, total, sums,
    out, v, buf, fixes, lhs, halves, slopes, turned, sems,
):
    gy = lax.axis_index("gy")
    columns = buf.shape[2]
    rows = columns + EDGE
    odd = lax.rem(gy, 2) == 1
    frac_low, frac, frac_high, scale = (vectors[i : i + 1, :] for i in range(4))

    def strip(pick, f, r):
        at = pl.ds((3 * f + r) * nz, nz)
        return pick[0][at, :], pick[1][at, :]

    def own_first(f, r):
        a, b = strip((own_a, own_b), f, r)
        return jnp.where(odd, a, b)

    def own_last(f, r):
        a, b = strip((own_a, own_b), f, r)
        return jnp.where(odd, b, a)

    def from_low(f, r):
        a, b = strip((got_a, got_b), f, r)
        return jnp.where(odd, a, b)

    def from_high(f, r):
        a, b = strip((got_a, got_b), f, r)
        return jnp.where(odd, b, a)

    def compact(ref):
        return ref[pl.ds(3, columns), :].T[:nz]

    below_c = compact(below)
    total_c = compact(total)
    incl_c = below_c + compact(sums)
    lane_one = lambda vector, at: vector[:, at : at + 1]

    def climb(start, slopes, sign, fractions):
        level, made = start, []
        for slope, fraction in zip(slopes, fractions):
            made.append(fraction * total_c - (level + (0.5 * sign) * slope))
            level = level + sign * slope
        return made

    v_first = climb(below_c, [own_first(2, r) for r in range(3)], 1.0, [lane_one(frac, r) for r in range(3)])
    v_last = climb(incl_c, [own_last(2, 2 - q) for q in range(3)], -1.0, [lane_one(frac, LANES - 1 - q) for q in range(3)])
    v_low = climb(below_c, [from_low(2, 2 - q) for q in range(3)], -1.0, [lane_one(frac_low, LANES - 1 - q) for q in range(3)])
    v_high = climb(incl_c, [from_high(2, r) for r in range(3)], 1.0, [lane_one(frac_high, r) for r in range(3)])
    v_low = [jnp.where(gy > 0, x, 0.0) for x in v_low]
    v_high = [jnp.where(gy < last, x, 0.0) for x in v_high]
    weight_of = dict(CENTRAL)
    for i in (15, 16, 17, 18, 19, 20):
        fixes[pl.ds(i * nz, nz), :] = jnp.zeros((nz, LANES), F32)
    for c in range(3):
        for side in range(2):
            v_own, v_out = (v_first, v_low) if side == 0 else (v_last, v_high)
            for q in range(3):
                value = None
                for m in range(3 - q):
                    if c == 1:
                        field = v_out[m]
                    elif side == 0:
                        field = from_low(c // 2, 2 - m)
                    else:
                        field = from_high(c // 2, m)
                    weight = weight_of[q + m + 1] * (-1.0 if side == 0 else 1.0)
                    term = weight * ((v_own[q] + v_out[m]) * field)
                    value = term if value is None else value + term
                at = q if side == 0 else LANES - 1 - q
                if c == 0:
                    row = q if side == 0 else 23 - q
                else:
                    row = 6 * c - 3 + (3 + q if side == 0 else 2 - q)
                fixes[pl.ds(row * nz, nz), :] = value * lane_one(scale, at)

    below_v = below[...]
    total_v = total[...]
    below_h = below_v.astype(BF16).astype(F32)
    below_l = below_v - below_h
    total_h = total_v.astype(BF16).astype(F32)
    total_l = total_v - total_h
    quarter = iota((rows, LANES), 1) // nz
    first_half = jnp.where(
        quarter == 0,
        below_h,
        jnp.where(
            quarter == 1,
            pltpu.roll(below_l, nz, 1),
            jnp.where(quarter == 2, pltpu.roll(total_h, 2 * nz, 1), pltpu.roll(total_l, 3 * nz, 1)),
        ),
    )
    second_half = jnp.where(quarter == 0, total_h, jnp.where(quarter == 1, pltpu.roll(total_l, nz, 1), 0.0))
    both = jnp.concatenate([first_half, second_half], axis=1).astype(BF16).astype(F32)
    for k in range(rows // 8):
        block = both[8 * k : 8 * k + 8]
        lhs[pl.ds(16 * k, 16), :] = jnp.concatenate([block, block], axis=0).astype(BF16)
    frac_h = frac.astype(BF16).astype(F32)
    frac_l = frac - frac_h
    k_index = iota((2 * LANES, LANES), 0)
    base = jnp.where(
        k_index < 2 * nz,
        -1.0,
        jnp.where(k_index < LANES, jnp.broadcast_to(frac_h, (2 * LANES, LANES)), jnp.broadcast_to(frac_l, (2 * LANES, LANES))),
    ).astype(BF16)
    tall = rows // 8

    def make_v(g):
        chosen = []
        for pair in range(GROUP // 2):
            mask = masks[pl.ds(pl.multiple_of(8 * (g * GROUP + 2 * pair), 16), 16), :]
            chosen += [lhs[pl.ds(16 * k, 16), :] * mask for k in range(tall)]
        level = jnp.dot(jnp.concatenate(chosen, axis=0), base, preferred_element_type=F32)
        for p in range(GROUP):
            for k in range(tall):
                at = pl.ds(LOW + 8 * k, 8)
                row = 16 * (p // 2 * tall + k) + 8 * (p % 2)
                v[g * GROUP + p, at, :] = v0[g * GROUP + p, at, :] + level[row : row + 8]

    def make_halves(g):
        for p in range(GROUP):
            z = g * GROUP + p
            here = v[z, pl.ds(EDGE, columns), :]
            for i, factor in enumerate((None, here, pad[0, z, pl.ds(EDGE, columns), :], pad[1, z, pl.ds(EDGE, columns), :])):
                halves[pl.ds((4 * p + i) * columns, columns), :] = split(here if factor is None else here * factor)

    def make_slopes():
        slopes[...] = jnp.dot(halves[...], matrix[...], preferred_element_type=F32)

    zeros = jnp.zeros((LANES - 24, LANES), F32)

    def make_turned(g):
        for p in range(GROUP):
            z = g * GROUP + p
            low = fixes[pl.ds(z, 16, stride=nz), :]
            high = fixes[pl.ds(16 * nz + z, 8, stride=nz), :]
            turned[p] = jnp.concatenate([low, zeros, high], axis=0).T

    groups = nz // GROUP
    for g in (groups - 1, 0, 1, 2):
        make_v(g)
    make_halves(0)
    make_slopes()
    make_turned(0)
    make_halves(1)
    lane = iota((8, LANES), 1)
    at_edge = (lane < 3) | (lane >= LANES - 3)

    def complete(g):
        for k in range(columns // 8):
            r = EDGE + 8 * k
            at = pl.ds(8 * k, 8)
            metric = mh[pl.ds(r, 8), :]
            level, factor = {}, {}

            def v_at(g, p):
                if p not in level:
                    level[p] = v[wrapped(g * GROUP + p, nz), pl.ds(r, 8), :]
                return level[p]

            def span_factor(g, distance, p):
                if (distance, p) not in factor:
                    factor[distance, p] = gzs[distance - 1, wrapped(g * GROUP + p, nz), at, :]
                return factor[distance, p]

            for p in range(GROUP):
                z = g * GROUP + p
                here = v_at(g, p)
                edge = turned[p, at, :]
                fix = [edge, pltpu.roll(edge, LANES - 6, 1), pltpu.roll(edge, LANES - 12, 1)]
                fix = [jnp.where(at_edge, x, 0.0) for x in fix]
                d_v, d_vv, d_vu, d_vw = (slopes[pl.ds((4 * p + i) * columns + 8 * k, 8), :] for i in range(4))
                buf[0, z, at, :] = part[0, z, at, :] + here * dwall[0, z, at, :] + (scale * d_vu + fix[0])
                buf[2, z, at, :] = part[1, z, at, :] + here * dwall[1, z, at, :] + (scale * d_vw + fix[2])
                across = along = None
                for distance, _w in CENTRAL:
                    a = gxs[distance - 1, z, pl.ds(r, 8), :] * v[z, pl.ds(r + distance, 8), :]
                    a = a - gxs[distance - 1, z, pl.ds(r - distance, 8), :] * v[z, pl.ds(r - distance, 8), :]
                    b = span_factor(g, distance, p) * v_at(g, p + distance)
                    b = b - span_factor(g, distance, p - distance) * v_at(g, p - distance)
                    across = a if across is None else across + a
                    along = b if along is None else along + b
                wallward = scale * (here * d_v + d_vv) + fix[1]
                buf[1, z, at, :] = across * metric + along + wallward

    def send(g):
        planes = pl.ds(g * GROUP, GROUP)
        return pltpu.make_async_copy(buf.at[:, planes], out.at[:, planes], sems.at[g])

    def step(g, _):
        complete(g)
        make_slopes()
        make_turned(wrapped(g + 1, groups))
        make_halves(wrapped(g + 2, groups))
        make_v(wrapped(g + 3, groups))
        send(g).start()
        return 0

    lax.fori_loop(0, groups, step, 0)
    for g in range(groups):
        send(g).wait()


def call(body, name, inputs, outputs, scratch, flops, moved, limit, far=(), aliases=None):
    return pl.pallas_call(
        body,
        name=name,
        in_specs=[HBM if i in far else WHOLE for i in range(len(inputs))],
        out_specs=tuple(HBM if isinstance(o, jax.ShapeDtypeStruct) else WHOLE for o in outputs),
        out_shape=tuple(outputs),
        scratch_shapes=scratch,
        input_output_aliases=aliases or {},
        cost_estimate=pl.CostEstimate(flops=flops, bytes_accessed=moved, transcendentals=0),
        compiler_params=pltpu.CompilerParams(vmem_limit_bytes=limit),
    )(*inputs)


def keep(*values):
    return [pltpu.with_memory_space_constraint(value, pltpu.VMEM) for value in values]


def shards(velocity, stream_metric, wall_metric):
    _, nz, columns, rows_here = velocity.shape
    n_gy = lax.axis_size("gy")
    last = n_gy - 1
    padded = columns + 2 * EDGE
    rows = columns + EDGE
    metric = stream_metric.reshape(2, columns)
    wall = wall_metric.reshape(n_gy, rows_here)
    volume = nz * columns * rows_here
    mib = 1 << 20
    vmem = lambda *shape: pltpu.VMEM(shape, F32)
    pad_shape = vmem(2, nz, padded, LANES)
    token_shape = vmem(rows, LANES)

    sent = jnp.concatenate([velocity[:, :, :EDGE], velocity[:, :, columns - EDGE :]], axis=2)
    xr = lax.ppermute(sent, "gx", [(0, 1), (1, 0)])

    near = pltpu.with_memory_space_constraint(velocity, pltpu.HBM)
    metric = pltpu.with_memory_space_constraint(metric, pltpu.HBM)
    wall = pltpu.with_memory_space_constraint(wall, pltpu.HBM)
    pad, uw, ms, mh, vectors, matrix, bits, masks = call(
        lambda *refs: sum_rows(nz, last, *refs),
        "sum_rows",
        (near, metric, wall),
        [pad_shape, vmem(columns, LANES), vmem(padded, LANES), vmem(padded, LANES), vmem(8, LANES), pltpu.VMEM((2 * LANES, LANES), BF16), vmem(8, LANES), pltpu.VMEM((8 * nz, 2 * LANES), BF16)],
        [vmem(2, columns), vmem(n_gy, rows_here), pltpu.SemaphoreType.DMA((10,))],
        4 * volume,
        8 * volume,
        2 * mib,
        far=(0, 1, 2),
    )
    pad, uw, ms, mh, vectors, matrix, masks = keep(pad, uw, ms, mh, vectors, matrix, masks)
    (sums,) = call(
        lambda *refs: sum_slopes(nz, *refs),
        "sum_slopes",
        (xr, uw, ms, vectors),
        [vmem(rows, LANES)],
        [vmem(padded, LANES)],
        volume // 4,
        volume // 2,
        2 * mib,
    )

    def scan_step(level, total, below, token=None):
        came = lax.ppermute(total, "gy", [(i, i ^ (1 << level)) for i in range(n_gy)])
        below = below + came * bits[level : level + 1]
        total = total + came
        return (total if token is None else total + token), below, came

    half = lambda count: pltpu.VMEM((count, 2 * LANES), BF16)
    pad, v0, dwall, strip_a, strip_b, token = call(
        lambda *refs: prepare(nz, *refs),
        "prepare",
        (pad, xr, ms, vectors, matrix),
        [pad_shape, vmem(nz, padded, LANES), vmem(2, nz, columns, LANES), vmem(9 * nz, LANES), vmem(9 * nz, LANES), token_shape],
        [half(2 * LANES)] * 3
        + [half(GROUP * rows), half(GROUP * columns), half(GROUP * columns), vmem(GROUP, rows, LANES), vmem(GROUP, 24, LANES)],
        60 * volume,
        8 * volume,
        6 * mib,
        aliases={0: 0},
    )
    pad, v0, dwall = keep(pad, v0, dwall)
    total, below, came = scan_step(0, sums, jnp.zeros_like(sums), token)

    got_a = lax.ppermute(strip_a, "gy", [(i, i ^ 1) for i in range(n_gy)])
    got_b = lax.ppermute(strip_b, "gy", [(i, i + 1) if i % 2 else (i, i - 1) for i in range(1, last)])
    pad, part, gxs, gzs, token = call(
        lambda *refs: known_terms(nz, *refs),
        "known_terms",
        (pad, mh, came, came),
        [pad_shape, vmem(2, nz, columns, LANES), vmem(3, nz, padded, LANES), vmem(3, nz, columns, LANES), token_shape],
        [],
        80 * volume,
        8 * volume,
        4 * mib,
        aliases={0: 0},
    )
    pad, part, gxs, gzs = keep(pad, part, gxs, gzs)
    total, below, came = scan_step(1, total, below, token)

    level = 2
    while (1 << level) < n_gy:
        total, below, came = scan_step(level, total, below)
        level += 1

    (out,) = call(
        lambda *refs: finish(nz, last, *refs),
        "finish",
        (pad, v0, part, dwall, gxs, gzs, mh, vectors, matrix, masks, strip_a, strip_b, got_a, got_b, below, total, sums),
        [jax.ShapeDtypeStruct((3, nz, columns, rows_here), F32)],
        [
            vmem(nz, padded, LANES),
            vmem(3, nz, columns, LANES),
            vmem(24 * nz, LANES),
            half(2 * rows),
            half(4 * GROUP * columns),
            vmem(4 * GROUP * columns, LANES),
            vmem(GROUP, columns, LANES),
            pltpu.SemaphoreType.DMA((nz // GROUP,)),
        ],
        80 * volume,
        20 * volume,
        16 * mib,
    )
    return out


def solution(mesh):
    in_specs = (P(None, None, "gx", "gy"), P(), P())
    out_specs = P(None, None, "gx", "gy")
    return jax.shard_map(shards, mesh=mesh, in_specs=in_specs, out_specs=out_specs, check_vma=False)
```

```python
import jax
import jax.numpy as jnp
from jax import lax
from jax.experimental import pallas as pl
from jax.experimental.pallas import tpu as pltpu
from jax.sharding import PartitionSpec as P

F32 = jnp.float32
BF16 = jnp.bfloat16
HALF60 = 0.5 / 60.0
CENTRAL = ((1, 45.0), (2, -9.0), (3, 1.0))
WALL_ROWS = (
    {0: -110.0, 1: 180.0, 2: -90.0, 3: 20.0},
    {-1: -20.0, 0: -30.0, 1: 60.0, 2: -10.0},
    {-2: 5.0, -1: -40.0, 1: 40.0, 2: -5.0},
)
LANES = 128
GROUP = 4
EDGE = 8
LOW = EDGE - 3

WHOLE = pl.BlockSpec(memory_space=pltpu.VMEM)
HBM = pl.BlockSpec(memory_space=pltpu.HBM)


def iota(shape, dim):
    return lax.broadcasted_iota(jnp.int32, shape, dim)


def split(value):
    high = value.astype(BF16)
    low = (value - high.astype(F32)).astype(BF16)
    return jnp.concatenate([high, low], axis=1)


def wrapped(plane, nz):
    return lax.rem(plane + nz, nz)


def wall_matrix(place, last):
    h = iota((LANES, LANES), 0)
    j = iota((LANES, LANES), 1)
    away = h - j
    inner = jnp.zeros((LANES, LANES), F32)
    for distance, weight in CENTRAL:
        inner = jnp.where(away == distance, weight, inner)
        inner = jnp.where(away == -distance, -weight, inner)
    for row, entries in enumerate(WALL_ROWS):
        for side in (0, 1):
            at = row if side == 0 else LANES - 1 - row
            sign = 1 if side == 0 else -1
            closed = jnp.zeros((LANES, LANES), F32)
            for offset, weight in entries.items():
                closed = jnp.where(away == sign * offset, sign * weight, closed)
            here = jnp.where(place == (0 if side == 0 else last), 1, 0)
            inner = jnp.where((j == at) & (here == 1), closed, inner)
    inner = inner.astype(BF16)
    return jnp.concatenate([inner, inner], axis=0)


def heights(wall, block, blocks):
    cell = 1.0 / wall[...]
    row = iota(cell.shape, 0)
    total = jnp.sum(cell)
    before = jnp.sum(jnp.where(row < block, cell, 0.0))
    mine = 1.0 / wall[pl.ds(block, 1), :]
    prefix = mine
    lane = iota((1, LANES), 1)
    for shift in (1, 2, 4, 8, 16, 32, 64):
        prefix = prefix + jnp.where(lane >= shift, pltpu.roll(prefix, shift, 1), 0.0)
    return (before + prefix - 0.5 * mine) / total


def sum_rows(nz, last, vel, metric_hbm, wall_hbm, pad, uw, ms, mh, vectors, matrix, bits, masks, metric, wall, sems):
    gx = lax.axis_index("gx")
    gy = lax.axis_index("gy")
    columns = uw.shape[0]
    chunks = 4
    per = nz // chunks

    def chunk(c):
        planes = pl.ds(c * per, per)
        return pltpu.make_async_copy(vel.at[:, planes], pad.at[:, planes, pl.ds(EDGE, columns)], sems.at[c])

    small = [
        pltpu.make_async_copy(wall_hbm, wall, sems.at[chunks]),
        pltpu.make_async_copy(metric_hbm, metric, sems.at[chunks + 1]),
    ]
    for copy in small:
        copy.start()
    for c in range(chunks):
        chunk(c).start()
    matrix[...] = wall_matrix(gy, last)
    plane = iota(masks.shape, 0) // 8
    masks[...] = jnp.where(lax.rem(iota(masks.shape, 1), nz) == plane, 1.0, 0.0).astype(BF16)
    for copy in small:
        copy.wait()
    own = jnp.broadcast_to(metric[pl.ds(gx, 1), :], (LANES, columns)).T
    peer = jnp.broadcast_to(metric[pl.ds(1 - gx, 1), :], (LANES, columns)).T
    ms[0:EDGE, :] = peer[columns - EDGE :]
    ms[EDGE : EDGE + columns, :] = own
    ms[EDGE + columns :, :] = peer[:EDGE]
    mh[...] = ms[...] * HALF60
    wall_here = wall[pl.ds(gy, 1), :]
    rw = 1.0 / wall_here
    vectors[0:1, :] = heights(wall, jnp.maximum(gy - 1, 0), last + 1)
    vectors[1:2, :] = heights(wall, gy, last + 1)
    vectors[2:3, :] = heights(wall, jnp.minimum(gy + 1, last), last + 1)
    vectors[3:4, :] = wall_here * HALF60
    vectors[4:5, :] = rw
    vectors[5:8, :] = jnp.zeros((3, LANES), F32)
    for i in range(bits.shape[0]):
        bits[i : i + 1, :] = jnp.full((1, LANES), jnp.where((gy & (1 << i)) != 0, 1.0, 0.0), F32)
    lane = iota((columns, LANES), 1)

    def group(g, held):
        chunk(g).wait()
        for p in range(per):
            z = g * per + p
            for c in range(2):
                line = jnp.sum(pad[c, z, pl.ds(EDGE, columns), :] * rw, axis=1, keepdims=True)
                held = jnp.where(lane == z + c * nz, line, held)
        return held

    uw[...] = lax.fori_loop(0, chunks, group, jnp.zeros((columns, LANES), F32))


def sum_slopes(nz, xr, uw, ms, vectors, sums, wide):
    columns = uw.shape[0]
    rows = columns + EDGE
    rw = vectors[4:5, :]
    lane = iota((2 * EDGE, LANES), 1)
    held = jnp.zeros((2 * EDGE, LANES), F32)
    for z in range(nz):
        for c in range(2):
            line = jnp.sum(xr[c, z] * rw, axis=1, keepdims=True)
            held = jnp.where(lane == z + c * nz, line, held)
    wide[0:EDGE, :] = held[EDGE:]
    wide[EDGE : EDGE + columns, :] = uw[...]
    wide[EDGE + columns :, :] = held[:EDGE]
    centre = wide[pl.ds(LOW, rows), :]
    lane = iota((rows, LANES), 1)
    around = jnp.where(lane < nz, pltpu.roll(centre, LANES - nz, 1), centre)
    around = jnp.where(lane < 2 * nz, around, pltpu.roll(around, 2 * nz, 1))
    du = dw = None
    for distance, weight in CENTRAL:
        a = weight * (wide[pl.ds(LOW + distance, rows), :] - wide[pl.ds(LOW - distance, rows), :])
        b = weight * (pltpu.roll(around, LANES - distance, 1) - pltpu.roll(around, distance, 1))
        du = a if du is None else du + a
        dw = b if dw is None else dw + b
    total = (ms[pl.ds(LOW, rows), :] * du + dw) * (1.0 / 60.0)
    sums[...] = jnp.where(lane < nz, total, 0.0)


def edge_columns(first_lane):
    h = iota((LANES, LANES), 0)
    lane = iota((LANES, LANES), 1) - first_lane
    last = (lane >= 0) & (lane < 3) & (h == lane + LANES - 3)
    first = (lane >= 3) & (lane < 6) & (h == lane - 3)
    picked = jnp.where(last | first, 1.0, 0.0).astype(BF16)
    return jnp.concatenate([picked, picked], axis=0)


def prepare(
    nz, first, count, pad, ms, vectors, matrix, v0, dwall, strip_a, strip_b, token,
    weights_s, weights_u, weights_w, halves_s, halves_u, halves_w, edges, turned,
):
    gy = lax.axis_index("gy")
    columns = dwall.shape[2]
    rows = columns + EDGE
    tall = rows // 8
    rw60 = vectors[4:5, :] * (1.0 / 60.0)
    scale = vectors[3:4, :]
    h = iota((LANES, LANES), 0)
    j = iota((LANES, LANES), 1)
    climb = jnp.where(h < j, -1.0, jnp.where(h == j, -0.5, 0.0)).astype(BF16)
    weights_s[:, :LANES] = jnp.concatenate([climb, climb], axis=0)
    weights_s[:, LANES:] = edge_columns(12)
    weights_u[:, :LANES] = matrix[...]
    weights_u[:, LANES:] = edge_columns(0)
    weights_w[:, :LANES] = matrix[...]
    weights_w[:, LANES:] = edge_columns(6)
    odd = lax.rem(gy, 2) == 1
    token[...] = jnp.zeros(token.shape, F32)

    def gather(g):
        blocks = []
        for p in range(GROUP):
            z = g * GROUP + p
            ups = [wrapped(z + d, nz) for d in (1, 2, 3)]
            downs = [wrapped(z - d, nz) for d in (1, 2, 3)]
            for k in range(tall):
                r = LOW + 8 * k
                du = dw = None
                for distance, weight in CENTRAL:
                    a = pad[0, z, pl.ds(r + distance, 8), :] - pad[0, z, pl.ds(r - distance, 8), :]
                    b = pad[1, ups[distance - 1], pl.ds(r, 8), :] - pad[1, downs[distance - 1], pl.ds(r, 8), :]
                    if weight != 1.0:
                        a, b = weight * a, weight * b
                    du = a if du is None else du + a
                    dw = b if dw is None else dw + b
                blocks.append((ms[pl.ds(r, 8), :] * du + dw) * rw60)
                if len(blocks) == 2:
                    halves_s[pl.ds(8 * (p * tall + k - 1), 16), :] = split(jnp.concatenate(blocks, axis=0))
                    blocks = []
            halves_u[pl.ds(p * columns, columns), :] = split(pad[0, z, pl.ds(EDGE, columns), :])
            halves_w[pl.ds(p * columns, columns), :] = split(pad[1, z, pl.ds(EDGE, columns), :])

    def settle(g):
        made_s = jnp.dot(halves_s[...], weights_s[...], preferred_element_type=F32)
        for p in range(GROUP):
            here = made_s[p * rows : (p + 1) * rows]
            v0[g * GROUP + p, pl.ds(LOW, rows), :] = here[:, :LANES]
            edges[p] = here[:, LANES:]
        made_u = jnp.dot(halves_u[...], weights_u[...], preferred_element_type=F32)
        made_w = jnp.dot(halves_w[...], weights_w[...], preferred_element_type=F32)
        for p in range(GROUP):
            z = g * GROUP + p
            at = slice(p * columns, (p + 1) * columns)
            dwall[0, z] = made_u[at, :LANES] * scale
            dwall[1, z] = made_w[at, :LANES] * scale
            packed = made_u[at, LANES:] + made_w[at, LANES:] + edges[p, pl.ds(3, columns), :]
            turned[p] = packed.T[:24]
            for f in range(3):
                high = turned[p, 6 * f : 6 * f + 3, :]
                low = turned[p, 6 * f + 3 : 6 * f + 6, :]
                strip_a[pl.ds(3 * f * nz + z, 3, stride=nz), :] = jnp.where(odd, low, high)
                strip_b[pl.ds(3 * f * nz + z, 3, stride=nz), :] = jnp.where(odd, high, low)

    def step(g, _):
        settle(g)
        gather(g + 1)
        return 0

    gather(first)
    lax.fori_loop(first, first + count - 1, step, 0)
    settle(first + count - 1)


def prepare_first(nz, first, count, pad_in, xr, ms, vectors, matrix, pad, *rest):
    del pad_in
    columns = pad.shape[2] - 2 * EDGE
    pad[:, :, pl.ds(0, EDGE), :] = xr[:, :, pl.ds(EDGE, EDGE), :]
    pad[:, :, pl.ds(EDGE + columns, EDGE), :] = xr[:, :, pl.ds(0, EDGE), :]
    prepare(nz, first, count, pad, ms, vectors, matrix, *rest)


def prepare_last(nz, first, count, pad, v0, dwall, strip_a, strip_b, ms, vectors, matrix, wait, *rest):
    del v0, dwall, strip_a, strip_b, wait
    prepare(nz, first, count, pad, ms, vectors, matrix, *rest)


def known_first(nz, count, pad, mh, wait, part, gx_out, gz_out, token):
    del wait
    for z in range(nz):
        u = pad[0, z, pl.ds(0, 8), :]
        for distance, weight in CENTRAL:
            gx_out[distance - 1, z, pl.ds(0, 8), :] = weight * (u + pad[0, z, pl.ds(distance, 8), :])
    known_terms(nz, 0, count, pad, mh, part, gx_out, gz_out, token)


def known_last(nz, first, pad, part_in, gx_in, gz_in, mh, wait_a, wait_b, wait_c, part, gx_out, gz_out, token):
    del part_in, gx_in, gz_in, wait_a, wait_b, wait_c
    known_terms(nz, first, part.shape[2] // 8 - first, pad, mh, part, gx_out, gz_out, token)


def known_terms(nz, first, count, pad, mh, part, gx_out, gz_out, token):
    token[...] = jnp.zeros(token.shape, F32)

    def block(k, _):
        r = pl.multiple_of(8 * k + EDGE, 8)
        at = pl.ds(pl.multiple_of(8 * k, 8), 8)
        metric = mh[pl.ds(r, 8), :]
        field = [{}, {}]
        factor = {}

        def load(c, z):
            if z not in field[c]:
                field[c][z] = pad[c, z % nz, pl.ds(r, 8), :]
            return field[c][z]

        def span_factor(distance, weight, z):
            if (distance, z) not in factor:
                factor[distance, z] = (load(1, z) + load(1, z + distance)) * (weight * HALF60)
            return factor[distance, z]

        for z in range(nz):
            u = load(0, z)
            across = [None, None]
            along = [None, None]
            for distance, weight in CENTRAL:
                ahead = [pad[c, z, pl.ds(r + distance, 8), :] for c in range(2)]
                behind = [pad[c, z, pl.ds(r - distance, 8), :] for c in range(2)]
                g, g_low = u + ahead[0], u + behind[0]
                if weight != 1.0:
                    g, g_low = weight * g, weight * g_low
                gx_out[distance - 1, z, pl.ds(r, 8), :] = g
                s = span_factor(distance, weight, z)
                s_low = span_factor(distance, weight, z - distance)
                gz_out[distance - 1, z, at, :] = s
                for c in range(2):
                    a = g * ahead[c] - g_low * behind[c]
                    b = s * load(c, z + distance) - s_low * load(c, z - distance)
                    across[c] = a if across[c] is None else across[c] + a
                    along[c] = b if along[c] is None else along[c] + b
            for c in range(2):
                part[c, z, at, :] = across[c] * metric + along[c]
        return 0

    lax.fori_loop(first, first + count, block, 0)


def finish(
    nz, last, pad, v0, part, dwall, gxs, gzs, mh, vectors, matrix, masks, own_a, own_b, got_a, got_b, below, total, sums,
    out, v, buf, fixes, lhs, halves, slopes, turned, sems,
):
    gy = lax.axis_index("gy")
    columns = buf.shape[2]
    rows = columns + EDGE
    odd = lax.rem(gy, 2) == 1
    frac_low, frac, frac_high, scale = (vectors[i : i + 1, :] for i in range(4))

    def strip(pick, f, r):
        at = pl.ds((3 * f + r) * nz, nz)
        return pick[0][at, :], pick[1][at, :]

    def own_first(f, r):
        a, b = strip((own_a, own_b), f, r)
        return jnp.where(odd, a, b)

    def own_last(f, r):
        a, b = strip((own_a, own_b), f, r)
        return jnp.where(odd, b, a)

    def from_low(f, r):
        a, b = strip((got_a, got_b), f, r)
        return jnp.where(odd, a, b)

    def from_high(f, r):
        a, b = strip((got_a, got_b), f, r)
        return jnp.where(odd, b, a)

    def compact(ref):
        return ref[pl.ds(3, columns), :].T[:nz]

    below_c = compact(below)
    total_c = compact(total)
    incl_c = below_c + compact(sums)
    lane_one = lambda vector, at: vector[:, at : at + 1]

    def climb(start, slopes, sign, fractions):
        level, made = start, []
        for slope, fraction in zip(slopes, fractions):
            made.append(fraction * total_c - (level + (0.5 * sign) * slope))
            level = level + sign * slope
        return made

    v_first = climb(below_c, [own_first(2, r) for r in range(3)], 1.0, [lane_one(frac, r) for r in range(3)])
    v_last = climb(incl_c, [own_last(2, 2 - q) for q in range(3)], -1.0, [lane_one(frac, LANES - 1 - q) for q in range(3)])
    v_low = climb(below_c, [from_low(2, 2 - q) for q in range(3)], -1.0, [lane_one(frac_low, LANES - 1 - q) for q in range(3)])
    v_high = climb(incl_c, [from_high(2, r) for r in range(3)], 1.0, [lane_one(frac_high, r) for r in range(3)])
    v_low = [jnp.where(gy > 0, x, 0.0) for x in v_low]
    v_high = [jnp.where(gy < last, x, 0.0) for x in v_high]
    weight_of = dict(CENTRAL)
    for i in (15, 16, 17, 18, 19, 20):
        fixes[pl.ds(i * nz, nz), :] = jnp.zeros((nz, LANES), F32)
    for c in range(3):
        for side in range(2):
            v_own, v_out = (v_first, v_low) if side == 0 else (v_last, v_high)
            for q in range(3):
                value = None
                for m in range(3 - q):
                    if c == 1:
                        field = v_out[m]
                    elif side == 0:
                        field = from_low(c // 2, 2 - m)
                    else:
                        field = from_high(c // 2, m)
                    weight = weight_of[q + m + 1] * (-1.0 if side == 0 else 1.0)
                    term = weight * ((v_own[q] + v_out[m]) * field)
                    value = term if value is None else value + term
                at = q if side == 0 else LANES - 1 - q
                if c == 0:
                    row = q if side == 0 else 23 - q
                else:
                    row = 6 * c - 3 + (3 + q if side == 0 else 2 - q)
                fixes[pl.ds(row * nz, nz), :] = value * lane_one(scale, at)

    below_v = below[...]
    total_v = total[...]
    below_h = below_v.astype(BF16).astype(F32)
    below_l = below_v - below_h
    total_h = total_v.astype(BF16).astype(F32)
    total_l = total_v - total_h
    quarter = iota((rows, LANES), 1) // nz
    first_half = jnp.where(
        quarter == 0,
        below_h,
        jnp.where(
            quarter == 1,
            pltpu.roll(below_l, nz, 1),
            jnp.where(quarter == 2, pltpu.roll(total_h, 2 * nz, 1), pltpu.roll(total_l, 3 * nz, 1)),
        ),
    )
    second_half = jnp.where(quarter == 0, total_h, jnp.where(quarter == 1, pltpu.roll(total_l, nz, 1), 0.0))
    both = jnp.concatenate([first_half, second_half], axis=1).astype(BF16).astype(F32)
    for k in range(rows // 8):
        block = both[8 * k : 8 * k + 8]
        lhs[pl.ds(16 * k, 16), :] = jnp.concatenate([block, block], axis=0).astype(BF16)
    frac_h = frac.astype(BF16).astype(F32)
    frac_l = frac - frac_h
    k_index = iota((2 * LANES, LANES), 0)
    base = jnp.where(
        k_index < 2 * nz,
        -1.0,
        jnp.where(k_index < LANES, jnp.broadcast_to(frac_h, (2 * LANES, LANES)), jnp.broadcast_to(frac_l, (2 * LANES, LANES))),
    ).astype(BF16)
    tall = rows // 8

    def make_v(g):
        chosen = []
        for pair in range(GROUP // 2):
            mask = masks[pl.ds(pl.multiple_of(8 * (g * GROUP + 2 * pair), 16), 16), :]
            chosen += [lhs[pl.ds(16 * k, 16), :] * mask for k in range(tall)]
        level = jnp.dot(jnp.concatenate(chosen, axis=0), base, preferred_element_type=F32)
        for p in range(GROUP):
            for k in range(tall):
                at = pl.ds(LOW + 8 * k, 8)
                row = 16 * (p // 2 * tall + k) + 8 * (p % 2)
                v[g * GROUP + p, at, :] = v0[g * GROUP + p, at, :] + level[row : row + 8]

    def make_halves(g):
        for p in range(GROUP):
            z = g * GROUP + p
            here = v[z, pl.ds(EDGE, columns), :]
            for i, factor in enumerate((None, here, pad[0, z, pl.ds(EDGE, columns), :], pad[1, z, pl.ds(EDGE, columns), :])):
                halves[pl.ds((4 * p + i) * columns, columns), :] = split(here if factor is None else here * factor)

    def make_slopes():
        slopes[...] = jnp.dot(halves[...], matrix[...], preferred_element_type=F32)

    zeros = jnp.zeros((LANES - 24, LANES), F32)

    def make_turned(g):
        for p in range(GROUP):
            z = g * GROUP + p
            low = fixes[pl.ds(z, 16, stride=nz), :]
            high = fixes[pl.ds(16 * nz + z, 8, stride=nz), :]
            turned[p] = jnp.concatenate([low, zeros, high], axis=0).T

    groups = nz // GROUP
    for g in (groups - 1, 0, 1, 2):
        make_v(g)
    make_halves(0)
    make_slopes()
    make_turned(0)
    make_halves(1)
    lane = iota((8, LANES), 1)
    at_edge = (lane < 3) | (lane >= LANES - 3)

    def complete(g):
        for k in range(columns // 8):
            r = EDGE + 8 * k
            at = pl.ds(8 * k, 8)
            metric = mh[pl.ds(r, 8), :]
            level, factor = {}, {}

            def v_at(g, p):
                if p not in level:
                    level[p] = v[wrapped(g * GROUP + p, nz), pl.ds(r, 8), :]
                return level[p]

            def span_factor(g, distance, p):
                if (distance, p) not in factor:
                    factor[distance, p] = gzs[distance - 1, wrapped(g * GROUP + p, nz), at, :]
                return factor[distance, p]

            for p in range(GROUP):
                z = g * GROUP + p
                here = v_at(g, p)
                edge = turned[p, at, :]
                fix = [edge, pltpu.roll(edge, LANES - 6, 1), pltpu.roll(edge, LANES - 12, 1)]
                fix = [jnp.where(at_edge, x, 0.0) for x in fix]
                d_v, d_vv, d_vu, d_vw = (slopes[pl.ds((4 * p + i) * columns + 8 * k, 8), :] for i in range(4))
                buf[0, z, at, :] = part[0, z, at, :] + here * dwall[0, z, at, :] + (scale * d_vu + fix[0])
                buf[2, z, at, :] = part[1, z, at, :] + here * dwall[1, z, at, :] + (scale * d_vw + fix[2])
                across = along = None
                for distance, _w in CENTRAL:
                    a = gxs[distance - 1, z, pl.ds(r, 8), :] * v[z, pl.ds(r + distance, 8), :]
                    a = a - gxs[distance - 1, z, pl.ds(r - distance, 8), :] * v[z, pl.ds(r - distance, 8), :]
                    b = span_factor(g, distance, p) * v_at(g, p + distance)
                    b = b - span_factor(g, distance, p - distance) * v_at(g, p - distance)
                    across = a if across is None else across + a
                    along = b if along is None else along + b
                wallward = scale * (here * d_v + d_vv) + fix[1]
                buf[1, z, at, :] = across * metric + along + wallward

    def send(g):
        planes = pl.ds(g * GROUP, GROUP)
        return pltpu.make_async_copy(buf.at[:, planes], out.at[:, planes], sems.at[g])

    def step(g, _=None, ahead=3):
        complete(g)
        send(g).start()
        if ahead > 0:
            make_slopes()
            make_turned(g + 1)
        if ahead > 1:
            make_halves(g + 2)
        if ahead > 2:
            make_v(g + 3)
        return 0

    for g in range(groups - 4):
        step(g)
    for g, ahead in ((groups - 4, 2), (groups - 3, 2), (groups - 2, 1), (groups - 1, 0)):
        step(g, ahead=ahead)
    for g in range(groups):
        send(g).wait()


def call(body, name, inputs, outputs, scratch, flops, moved, limit, far=(), aliases=None):
    return pl.pallas_call(
        body,
        name=name,
        in_specs=[HBM if i in far else WHOLE for i in range(len(inputs))],
        out_specs=tuple(HBM if isinstance(o, jax.ShapeDtypeStruct) else WHOLE for o in outputs),
        out_shape=tuple(outputs),
        scratch_shapes=scratch,
        input_output_aliases=aliases or {},
        cost_estimate=pl.CostEstimate(flops=flops, bytes_accessed=moved, transcendentals=0),
        compiler_params=pltpu.CompilerParams(vmem_limit_bytes=limit),
    )(*inputs)


def keep(*values):
    return [pltpu.with_memory_space_constraint(value, pltpu.VMEM) for value in values]


def shards(velocity, stream_metric, wall_metric):
    _, nz, columns, rows_here = velocity.shape
    n_gy = lax.axis_size("gy")
    last = n_gy - 1
    padded = columns + 2 * EDGE
    rows = columns + EDGE
    metric = stream_metric.reshape(2, columns)
    wall = wall_metric.reshape(n_gy, rows_here)
    volume = nz * columns * rows_here
    mib = 1 << 20
    vmem = lambda *shape: pltpu.VMEM(shape, F32)
    pad_shape = vmem(2, nz, padded, LANES)
    token_shape = vmem(rows, LANES)

    sent = jnp.concatenate([velocity[:, :, :EDGE], velocity[:, :, columns - EDGE :]], axis=2)
    xr = lax.ppermute(sent, "gx", [(0, 1), (1, 0)])

    near = pltpu.with_memory_space_constraint(velocity, pltpu.HBM)
    metric = pltpu.with_memory_space_constraint(metric, pltpu.HBM)
    wall = pltpu.with_memory_space_constraint(wall, pltpu.HBM)
    pad, uw, ms, mh, vectors, matrix, bits, masks = call(
        lambda *refs: sum_rows(nz, last, *refs),
        "sum_rows",
        (near, metric, wall),
        [pad_shape, vmem(columns, LANES), vmem(padded, LANES), vmem(padded, LANES), vmem(8, LANES), pltpu.VMEM((2 * LANES, LANES), BF16), vmem(8, LANES), pltpu.VMEM((8 * nz, 2 * LANES), BF16)],
        [vmem(2, columns), vmem(n_gy, rows_here), pltpu.SemaphoreType.DMA((6,))],
        4 * volume,
        8 * volume,
        2 * mib,
        far=(0, 1, 2),
    )
    pad, uw, ms, mh, vectors, matrix, masks = keep(pad, uw, ms, mh, vectors, matrix, masks)
    (sums,) = call(
        lambda *refs: sum_slopes(nz, *refs),
        "sum_slopes",
        (xr, uw, ms, vectors),
        [vmem(rows, LANES)],
        [vmem(padded, LANES)],
        volume // 4,
        volume // 2,
        2 * mib,
    )

    def scan_step(level, total, below, token=None):
        came = lax.ppermute(total, "gy", [(i, i ^ (1 << level)) for i in range(n_gy)])
        below = below + came * bits[level : level + 1]
        total = total + came
        return (total if token is None else total + token), below, came

    half = lambda count: pltpu.VMEM((count, 2 * LANES), BF16)
    groups = nz // GROUP
    blocks = columns // 8
    first_groups, first_blocks = groups // 2, blocks // 2
    half = lambda count: pltpu.VMEM((count, 2 * LANES), BF16)
    prepared = [vmem(nz, padded, LANES), vmem(2, nz, columns, LANES), vmem(9 * nz, LANES), vmem(9 * nz, LANES), token_shape]
    prepare_scratch = [half(2 * LANES)] * 3 + [
        half(GROUP * rows),
        half(GROUP * columns),
        half(GROUP * columns),
        vmem(GROUP, rows, LANES),
        vmem(GROUP, 24, LANES),
    ]
    pad, v0, dwall, strip_a, strip_b, token = call(
        lambda *refs: prepare_first(nz, 0, first_groups, *refs),
        "prepare_first",
        (pad, xr, ms, vectors, matrix),
        [pad_shape] + prepared,
        prepare_scratch,
        30 * volume,
        4 * volume,
        6 * mib,
        aliases={0: 0},
    )
    pad, v0, dwall, strip_a, strip_b = keep(pad, v0, dwall, strip_a, strip_b)
    total, below, came = scan_step(0, sums, jnp.zeros_like(sums), token)
    v0, dwall, strip_a, strip_b, token = call(
        lambda *refs: prepare_last(nz, first_groups, groups - first_groups, *refs),
        "prepare_last",
        (pad, v0, dwall, strip_a, strip_b, ms, vectors, matrix, came),
        prepared,
        prepare_scratch,
        30 * volume,
        4 * volume,
        6 * mib,
        aliases={1: 0, 2: 1, 3: 2, 4: 3},
    )
    v0, dwall = keep(v0, dwall)
    total, below, came = scan_step(1, total, below, token)

    got_a = lax.ppermute(strip_a, "gy", [(i, i ^ 1) for i in range(n_gy)])
    got_b = lax.ppermute(strip_b, "gy", [(i, i + 1) if i % 2 else (i, i - 1) for i in range(1, last)])
    known = [vmem(2, nz, columns, LANES), vmem(3, nz, padded, LANES), vmem(3, nz, columns, LANES), token_shape]
    part, gxs, gzs, token = call(
        lambda *refs: known_first(nz, first_blocks, *refs),
        "known_first",
        (pad, mh, came),
        known,
        [],
        40 * volume,
        4 * volume,
        4 * mib,
    )
    part, gxs, gzs = keep(part, gxs, gzs)
    total, below, came = scan_step(2, total, below, token)
    part, gxs, gzs, token = call(
        lambda *refs: known_last(nz, first_blocks, *refs),
        "known_last",
        (pad, part, gxs, gzs, mh, came, got_a, got_b),
        known,
        [],
        40 * volume,
        4 * volume,
        4 * mib,
        aliases={1: 0, 2: 1, 3: 2},
    )
    part, gxs, gzs = keep(part, gxs, gzs)

    level = 3
    while (1 << level) < n_gy:
        total, below, came = scan_step(level, total, below)
        level += 1

    (out,) = call(
        lambda *refs: finish(nz, last, *refs),
        "finish",
        (pad, v0, part, dwall, gxs, gzs, mh, vectors, matrix, masks, strip_a, strip_b, got_a, got_b, below, total, sums),
        [jax.ShapeDtypeStruct((3, nz, columns, rows_here), F32)],
        [
            vmem(nz, padded, LANES),
            vmem(3, nz, columns, LANES),
            vmem(24 * nz, LANES),
            half(2 * rows),
            half(4 * GROUP * columns),
            vmem(4 * GROUP * columns, LANES),
            vmem(GROUP, columns, LANES),
            pltpu.SemaphoreType.DMA((nz // GROUP,)),
        ],
        80 * volume,
        20 * volume,
        16 * mib,
    )
    return out


def solution(mesh):
    in_specs = (P(None, None, "gx", "gy"), P(), P())
    out_specs = P(None, None, "gx", "gy")
    return jax.shard_map(shards, mesh=mesh, in_specs=in_specs, out_specs=out_specs, check_vma=False)
```

```python
import jax
import jax.numpy as jnp
from jax import lax
from jax.experimental import pallas as pl
from jax.experimental.pallas import tpu as pltpu
from jax.sharding import PartitionSpec as P

F32 = jnp.float32
BF16 = jnp.bfloat16
HALF60 = 0.5 / 60.0
CENTRAL = ((1, 45.0), (2, -9.0), (3, 1.0))
WALL_ROWS = (
    {0: -110.0, 1: 180.0, 2: -90.0, 3: 20.0},
    {-1: -20.0, 0: -30.0, 1: 60.0, 2: -10.0},
    {-2: 5.0, -1: -40.0, 1: 40.0, 2: -5.0},
)
LANES = 128
GROUP = 4
EDGE = 8
LOW = EDGE - 3

WHOLE = pl.BlockSpec(memory_space=pltpu.VMEM)
HBM = pl.BlockSpec(memory_space=pltpu.HBM)


def iota(shape, dim):
    return lax.broadcasted_iota(jnp.int32, shape, dim)


def split(value):
    high = value.astype(BF16)
    low = (value - high.astype(F32)).astype(BF16)
    return jnp.concatenate([high, low], axis=1)


def wrapped(plane, nz):
    return lax.rem(plane + nz, nz)


def wall_matrix(place, last):
    h = iota((LANES, LANES), 0)
    j = iota((LANES, LANES), 1)
    away = h - j
    inner = jnp.zeros((LANES, LANES), F32)
    for distance, weight in CENTRAL:
        inner = jnp.where(away == distance, weight, inner)
        inner = jnp.where(away == -distance, -weight, inner)
    for row, entries in enumerate(WALL_ROWS):
        for side in (0, 1):
            at = row if side == 0 else LANES - 1 - row
            sign = 1 if side == 0 else -1
            closed = jnp.zeros((LANES, LANES), F32)
            for offset, weight in entries.items():
                closed = jnp.where(away == sign * offset, sign * weight, closed)
            here = jnp.where(place == (0 if side == 0 else last), 1, 0)
            inner = jnp.where((j == at) & (here == 1), closed, inner)
    inner = inner.astype(BF16)
    return jnp.concatenate([inner, inner], axis=0)


def heights(wall, block, blocks):
    cell = 1.0 / wall[...]
    row = iota(cell.shape, 0)
    total = jnp.sum(cell)
    before = jnp.sum(jnp.where(row < block, cell, 0.0))
    mine = 1.0 / wall[pl.ds(block, 1), :]
    prefix = mine
    lane = iota((1, LANES), 1)
    for shift in (1, 2, 4, 8, 16, 32, 64):
        prefix = prefix + jnp.where(lane >= shift, pltpu.roll(prefix, shift, 1), 0.0)
    return (before + prefix - 0.5 * mine) / total


def sum_rows(nz, last, vel, metric_hbm, wall_hbm, pad, uw, ms, mh, vectors, matrix, bits, masks, metric, wall, sems):
    gx = lax.axis_index("gx")
    gy = lax.axis_index("gy")
    columns = uw.shape[0]
    chunks = 4
    per = nz // chunks

    def chunk(c):
        planes = pl.ds(c * per, per)
        return pltpu.make_async_copy(vel.at[:, planes], pad.at[:, planes, pl.ds(EDGE, columns)], sems.at[c])

    small = [
        pltpu.make_async_copy(wall_hbm, wall, sems.at[chunks]),
        pltpu.make_async_copy(metric_hbm, metric, sems.at[chunks + 1]),
    ]
    for copy in small:
        copy.start()
    for c in range(chunks):
        chunk(c).start()
    matrix[...] = wall_matrix(gy, last)
    plane = iota(masks.shape, 0) // 8
    masks[...] = jnp.where(lax.rem(iota(masks.shape, 1), nz) == plane, 1.0, 0.0).astype(BF16)
    for copy in small:
        copy.wait()
    own = jnp.broadcast_to(metric[pl.ds(gx, 1), :], (LANES, columns)).T
    peer = jnp.broadcast_to(metric[pl.ds(1 - gx, 1), :], (LANES, columns)).T
    ms[0:EDGE, :] = peer[columns - EDGE :]
    ms[EDGE : EDGE + columns, :] = own
    ms[EDGE + columns :, :] = peer[:EDGE]
    mh[...] = ms[...] * HALF60
    wall_here = wall[pl.ds(gy, 1), :]
    rw = 1.0 / wall_here
    vectors[0:1, :] = heights(wall, jnp.maximum(gy - 1, 0), last + 1)
    vectors[1:2, :] = heights(wall, gy, last + 1)
    vectors[2:3, :] = heights(wall, jnp.minimum(gy + 1, last), last + 1)
    vectors[3:4, :] = wall_here * HALF60
    vectors[4:5, :] = rw
    vectors[5:8, :] = jnp.zeros((3, LANES), F32)
    for i in range(bits.shape[0]):
        bits[i : i + 1, :] = jnp.full((1, LANES), jnp.where((gy & (1 << i)) != 0, 1.0, 0.0), F32)
    lane = iota((columns, LANES), 1)

    def group(g, held):
        chunk(g).wait()
        for p in range(per):
            z = g * per + p
            for c in range(2):
                line = jnp.sum(pad[c, z, pl.ds(EDGE, columns), :] * rw, axis=1, keepdims=True)
                held = jnp.where(lane == z + c * nz, line, held)
        return held

    uw[...] = lax.fori_loop(0, chunks, group, jnp.zeros((columns, LANES), F32))


def sum_slopes(nz, xr, uw, ms, vectors, sums, wide):
    columns = uw.shape[0]
    rows = columns + EDGE
    rw = vectors[4:5, :]
    lane = iota((2 * EDGE, LANES), 1)
    held = jnp.zeros((2 * EDGE, LANES), F32)
    for z in range(nz):
        for c in range(2):
            line = jnp.sum(xr[c, z] * rw, axis=1, keepdims=True)
            held = jnp.where(lane == z + c * nz, line, held)
    wide[0:EDGE, :] = held[EDGE:]
    wide[EDGE : EDGE + columns, :] = uw[...]
    wide[EDGE + columns :, :] = held[:EDGE]
    centre = wide[pl.ds(LOW, rows), :]
    lane = iota((rows, LANES), 1)
    around = jnp.where(lane < nz, pltpu.roll(centre, LANES - nz, 1), centre)
    around = jnp.where(lane < 2 * nz, around, pltpu.roll(around, 2 * nz, 1))
    du = dw = None
    for distance, weight in CENTRAL:
        a = weight * (wide[pl.ds(LOW + distance, rows), :] - wide[pl.ds(LOW - distance, rows), :])
        b = weight * (pltpu.roll(around, LANES - distance, 1) - pltpu.roll(around, distance, 1))
        du = a if du is None else du + a
        dw = b if dw is None else dw + b
    total = (ms[pl.ds(LOW, rows), :] * du + dw) * (1.0 / 60.0)
    sums[...] = jnp.where(lane < nz, total, 0.0)


def edge_columns(first_lane):
    h = iota((LANES, LANES), 0)
    lane = iota((LANES, LANES), 1) - first_lane
    last = (lane >= 0) & (lane < 3) & (h == lane + LANES - 3)
    first = (lane >= 3) & (lane < 6) & (h == lane - 3)
    picked = jnp.where(last | first, 1.0, 0.0).astype(BF16)
    return jnp.concatenate([picked, picked], axis=0)


def prepare(
    nz, first, count, pad, ms, vectors, matrix, v0, dwall, strip_a, strip_b, token,
    weights_s, weights_u, weights_w, halves_s, halves_u, halves_w, edges, turned,
):
    gy = lax.axis_index("gy")
    columns = dwall.shape[2]
    rows = columns + EDGE
    tall = rows // 8
    rw60 = vectors[4:5, :] * (1.0 / 60.0)
    scale = vectors[3:4, :]
    h = iota((LANES, LANES), 0)
    j = iota((LANES, LANES), 1)
    climb = jnp.where(h < j, -1.0, jnp.where(h == j, -0.5, 0.0)).astype(BF16)
    weights_s[:, :LANES] = jnp.concatenate([climb, climb], axis=0)
    weights_s[:, LANES:] = edge_columns(12)
    weights_u[:, :LANES] = matrix[...]
    weights_u[:, LANES:] = edge_columns(0)
    weights_w[:, :LANES] = matrix[...]
    weights_w[:, LANES:] = edge_columns(6)
    odd = lax.rem(gy, 2) == 1
    token[...] = jnp.zeros(token.shape, F32)

    def gather(g):
        blocks = []
        for p in range(GROUP):
            z = g * GROUP + p
            ups = [wrapped(z + d, nz) for d in (1, 2, 3)]
            downs = [wrapped(z - d, nz) for d in (1, 2, 3)]
            for k in range(tall):
                r = LOW + 8 * k
                du = dw = None
                for distance, weight in CENTRAL:
                    a = pad[0, z, pl.ds(r + distance, 8), :] - pad[0, z, pl.ds(r - distance, 8), :]
                    b = pad[1, ups[distance - 1], pl.ds(r, 8), :] - pad[1, downs[distance - 1], pl.ds(r, 8), :]
                    if weight != 1.0:
                        a, b = weight * a, weight * b
                    du = a if du is None else du + a
                    dw = b if dw is None else dw + b
                blocks.append((ms[pl.ds(r, 8), :] * du + dw) * rw60)
                if len(blocks) == 2:
                    halves_s[pl.ds(8 * (p * tall + k - 1), 16), :] = split(jnp.concatenate(blocks, axis=0))
                    blocks = []
            halves_u[pl.ds(p * columns, columns), :] = split(pad[0, z, pl.ds(EDGE, columns), :])
            halves_w[pl.ds(p * columns, columns), :] = split(pad[1, z, pl.ds(EDGE, columns), :])

    def settle(g):
        made_s = jnp.dot(halves_s[...], weights_s[...], preferred_element_type=F32)
        for p in range(GROUP):
            here = made_s[p * rows : (p + 1) * rows]
            v0[g * GROUP + p, pl.ds(LOW, rows), :] = here[:, :LANES]
            edges[p] = here[:, LANES:]
        made_u = jnp.dot(halves_u[...], weights_u[...], preferred_element_type=F32)
        made_w = jnp.dot(halves_w[...], weights_w[...], preferred_element_type=F32)
        for p in range(GROUP):
            z = g * GROUP + p
            at = slice(p * columns, (p + 1) * columns)
            dwall[0, z] = made_u[at, :LANES] * scale
            dwall[1, z] = made_w[at, :LANES] * scale
            packed = made_u[at, LANES:] + made_w[at, LANES:] + edges[p, pl.ds(3, columns), :]
            turned[p] = packed.T[:24]
            for f in range(3):
                high = turned[p, 6 * f : 6 * f + 3, :]
                low = turned[p, 6 * f + 3 : 6 * f + 6, :]
                strip_a[pl.ds(3 * f * nz + z, 3, stride=nz), :] = jnp.where(odd, low, high)
                strip_b[pl.ds(3 * f * nz + z, 3, stride=nz), :] = jnp.where(odd, high, low)

    def step(g, _):
        settle(g)
        gather(g + 1)
        return 0

    gather(first)
    lax.fori_loop(first, first + count - 1, step, 0)
    settle(first + count - 1)


def prepare_first(nz, first, count, pad_in, xr, ms, vectors, matrix, pad, *rest):
    del pad_in
    columns = pad.shape[2] - 2 * EDGE
    pad[:, :, pl.ds(0, EDGE), :] = xr[:, :, pl.ds(EDGE, EDGE), :]
    pad[:, :, pl.ds(EDGE + columns, EDGE), :] = xr[:, :, pl.ds(0, EDGE), :]
    prepare(nz, first, count, pad, ms, vectors, matrix, *rest)


def prepare_last(nz, first, count, pad, v0, dwall, strip_a, strip_b, ms, vectors, matrix, wait, *rest):
    del v0, dwall, strip_a, strip_b, wait
    prepare(nz, first, count, pad, ms, vectors, matrix, *rest)


def known_first(nz, count, pad, mh, wait, part, gx_out, gz_out, token):
    del wait
    for z in range(nz):
        u = pad[0, z, pl.ds(0, 8), :]
        for distance, weight in CENTRAL:
            gx_out[distance - 1, z, pl.ds(0, 8), :] = weight * (u + pad[0, z, pl.ds(distance, 8), :])
    known_terms(nz, 0, count, pad, mh, part, gx_out, gz_out, token)


def known_last(nz, first, pad, part_in, gx_in, gz_in, mh, wait_a, wait_b, wait_c, part, gx_out, gz_out, token):
    del part_in, gx_in, gz_in, wait_a, wait_b, wait_c
    known_terms(nz, first, part.shape[2] // 8 - first, pad, mh, part, gx_out, gz_out, token)


def known_terms(nz, first, count, pad, mh, part, gx_out, gz_out, token):
    token[...] = jnp.zeros(token.shape, F32)

    def block(k, _):
        r = pl.multiple_of(8 * k + EDGE, 8)
        at = pl.ds(pl.multiple_of(8 * k, 8), 8)
        metric = mh[pl.ds(r, 8), :]
        field = [{}, {}]
        factor = {}

        def load(c, z):
            if z not in field[c]:
                field[c][z] = pad[c, z % nz, pl.ds(r, 8), :]
            return field[c][z]

        def span_factor(distance, weight, z):
            if (distance, z) not in factor:
                factor[distance, z] = (load(1, z) + load(1, z + distance)) * (weight * HALF60)
            return factor[distance, z]

        for z in range(nz):
            u = load(0, z)
            across = [None, None]
            along = [None, None]
            for distance, weight in CENTRAL:
                ahead = [pad[c, z, pl.ds(r + distance, 8), :] for c in range(2)]
                behind = [pad[c, z, pl.ds(r - distance, 8), :] for c in range(2)]
                g, g_low = u + ahead[0], u + behind[0]
                if weight != 1.0:
                    g, g_low = weight * g, weight * g_low
                gx_out[distance - 1, z, pl.ds(r, 8), :] = g
                s = span_factor(distance, weight, z)
                s_low = span_factor(distance, weight, z - distance)
                gz_out[distance - 1, z, at, :] = s
                for c in range(2):
                    a = g * ahead[c] - g_low * behind[c]
                    b = s * load(c, z + distance) - s_low * load(c, z - distance)
                    across[c] = a if across[c] is None else across[c] + a
                    along[c] = b if along[c] is None else along[c] + b
            for c in range(2):
                part[c, z, at, :] = across[c] * metric + along[c]
        return 0

    lax.fori_loop(first, first + count, block, 0)


def finish(
    nz, last, pad, v0, part, dwall, gxs, gzs, mh, vectors, matrix, masks, own_a, own_b, got_a, got_b, below, total, sums,
    out, v, buf, fixes, lhs, halves, slopes, turned, sems,
):
    gy = lax.axis_index("gy")
    columns = buf.shape[2]
    rows = columns + EDGE
    odd = lax.rem(gy, 2) == 1
    frac_low, frac, frac_high, scale = (vectors[i : i + 1, :] for i in range(4))

    def strip(pick, f, r):
        at = pl.ds((3 * f + r) * nz, nz)
        return pick[0][at, :], pick[1][at, :]

    def own_first(f, r):
        a, b = strip((own_a, own_b), f, r)
        return jnp.where(odd, a, b)

    def own_last(f, r):
        a, b = strip((own_a, own_b), f, r)
        return jnp.where(odd, b, a)

    def from_low(f, r):
        a, b = strip((got_a, got_b), f, r)
        return jnp.where(odd, a, b)

    def from_high(f, r):
        a, b = strip((got_a, got_b), f, r)
        return jnp.where(odd, b, a)

    def compact(ref):
        return ref[pl.ds(3, columns), :].T[:nz]

    below_c = compact(below)
    total_c = compact(total)
    incl_c = below_c + compact(sums)
    lane_one = lambda vector, at: vector[:, at : at + 1]

    def climb(start, slopes, sign, fractions):
        level, made = start, []
        for slope, fraction in zip(slopes, fractions):
            made.append(fraction * total_c - (level + (0.5 * sign) * slope))
            level = level + sign * slope
        return made

    v_first = climb(below_c, [own_first(2, r) for r in range(3)], 1.0, [lane_one(frac, r) for r in range(3)])
    v_last = climb(incl_c, [own_last(2, 2 - q) for q in range(3)], -1.0, [lane_one(frac, LANES - 1 - q) for q in range(3)])
    v_low = climb(below_c, [from_low(2, 2 - q) for q in range(3)], -1.0, [lane_one(frac_low, LANES - 1 - q) for q in range(3)])
    v_high = climb(incl_c, [from_high(2, r) for r in range(3)], 1.0, [lane_one(frac_high, r) for r in range(3)])
    v_low = [jnp.where(gy > 0, x, 0.0) for x in v_low]
    v_high = [jnp.where(gy < last, x, 0.0) for x in v_high]
    weight_of = dict(CENTRAL)
    for i in (15, 16, 17, 18, 19, 20):
        fixes[pl.ds(i * nz, nz), :] = jnp.zeros((nz, LANES), F32)
    for c in range(3):
        for side in range(2):
            v_own, v_out = (v_first, v_low) if side == 0 else (v_last, v_high)
            for q in range(3):
                value = None
                for m in range(3 - q):
                    if c == 1:
                        field = v_out[m]
                    elif side == 0:
                        field = from_low(c // 2, 2 - m)
                    else:
                        field = from_high(c // 2, m)
                    weight = weight_of[q + m + 1] * (-1.0 if side == 0 else 1.0)
                    term = weight * ((v_own[q] + v_out[m]) * field)
                    value = term if value is None else value + term
                at = q if side == 0 else LANES - 1 - q
                if c == 0:
                    row = q if side == 0 else 23 - q
                else:
                    row = 6 * c - 3 + (3 + q if side == 0 else 2 - q)
                fixes[pl.ds(row * nz, nz), :] = value * lane_one(scale, at)

    below_v = below[...]
    total_v = total[...]
    below_h = below_v.astype(BF16).astype(F32)
    below_l = below_v - below_h
    total_h = total_v.astype(BF16).astype(F32)
    total_l = total_v - total_h
    quarter = iota((rows, LANES), 1) // nz
    first_half = jnp.where(
        quarter == 0,
        below_h,
        jnp.where(
            quarter == 1,
            pltpu.roll(below_l, nz, 1),
            jnp.where(quarter == 2, pltpu.roll(total_h, 2 * nz, 1), pltpu.roll(total_l, 3 * nz, 1)),
        ),
    )
    second_half = jnp.where(quarter == 0, total_h, jnp.where(quarter == 1, pltpu.roll(total_l, nz, 1), 0.0))
    both = jnp.concatenate([first_half, second_half], axis=1).astype(BF16).astype(F32)
    for k in range(rows // 8):
        block = both[8 * k : 8 * k + 8]
        lhs[pl.ds(16 * k, 16), :] = jnp.concatenate([block, block], axis=0).astype(BF16)
    frac_h = frac.astype(BF16).astype(F32)
    frac_l = frac - frac_h
    k_index = iota((2 * LANES, LANES), 0)
    base = jnp.where(
        k_index < 2 * nz,
        -1.0,
        jnp.where(k_index < LANES, jnp.broadcast_to(frac_h, (2 * LANES, LANES)), jnp.broadcast_to(frac_l, (2 * LANES, LANES))),
    ).astype(BF16)
    tall = rows // 8

    def make_v(g):
        chosen = []
        for pair in range(GROUP // 2):
            mask = masks[pl.ds(pl.multiple_of(8 * (g * GROUP + 2 * pair), 16), 16), :]
            chosen += [lhs[pl.ds(16 * k, 16), :] * mask for k in range(tall)]
        level = jnp.dot(jnp.concatenate(chosen, axis=0), base, preferred_element_type=F32)
        for p in range(GROUP):
            for k in range(tall):
                at = pl.ds(LOW + 8 * k, 8)
                row = 16 * (p // 2 * tall + k) + 8 * (p % 2)
                v[g * GROUP + p, at, :] = v0[g * GROUP + p, at, :] + level[row : row + 8]

    def make_halves(g):
        for p in range(GROUP):
            z = g * GROUP + p
            here = v[z, pl.ds(EDGE, columns), :]
            for i, factor in enumerate((None, here, pad[0, z, pl.ds(EDGE, columns), :], pad[1, z, pl.ds(EDGE, columns), :])):
                halves[pl.ds((4 * p + i) * columns, columns), :] = split(here if factor is None else here * factor)

    def make_slopes():
        slopes[...] = jnp.dot(halves[...], matrix[...], preferred_element_type=F32)

    zeros = jnp.zeros((LANES - 24, LANES), F32)

    def make_turned(g):
        for p in range(GROUP):
            z = g * GROUP + p
            low = fixes[pl.ds(z, 16, stride=nz), :]
            high = fixes[pl.ds(16 * nz + z, 8, stride=nz), :]
            turned[p] = jnp.concatenate([low, zeros, high], axis=0).T

    groups = nz // GROUP
    for g in (groups - 1, 0, 1, 2):
        make_v(g)
    make_halves(0)
    make_slopes()
    make_turned(0)
    make_halves(1)
    lane = iota((8, LANES), 1)
    at_edge = (lane < 3) | (lane >= LANES - 3)

    def complete(g):
        for k in range(columns // 8):
            r = EDGE + 8 * k
            at = pl.ds(8 * k, 8)
            metric = mh[pl.ds(r, 8), :]
            level, factor = {}, {}

            def v_at(g, p):
                if p not in level:
                    level[p] = v[wrapped(g * GROUP + p, nz), pl.ds(r, 8), :]
                return level[p]

            def span_factor(g, distance, p):
                if (distance, p) not in factor:
                    factor[distance, p] = gzs[distance - 1, wrapped(g * GROUP + p, nz), at, :]
                return factor[distance, p]

            for p in range(GROUP):
                z = g * GROUP + p
                here = v_at(g, p)
                edge = turned[p, at, :]
                fix = [edge, pltpu.roll(edge, LANES - 6, 1), pltpu.roll(edge, LANES - 12, 1)]
                fix = [jnp.where(at_edge, x, 0.0) for x in fix]
                d_v, d_vv, d_vu, d_vw = (slopes[pl.ds((4 * p + i) * columns + 8 * k, 8), :] for i in range(4))
                buf[0, z, at, :] = part[0, z, at, :] + here * dwall[0, z, at, :] + (scale * d_vu + fix[0])
                buf[2, z, at, :] = part[1, z, at, :] + here * dwall[1, z, at, :] + (scale * d_vw + fix[2])
                across = along = None
                for distance, _w in CENTRAL:
                    a = gxs[distance - 1, z, pl.ds(r, 8), :] * v[z, pl.ds(r + distance, 8), :]
                    a = a - gxs[distance - 1, z, pl.ds(r - distance, 8), :] * v[z, pl.ds(r - distance, 8), :]
                    b = span_factor(g, distance, p) * v_at(g, p + distance)
                    b = b - span_factor(g, distance, p - distance) * v_at(g, p - distance)
                    across = a if across is None else across + a
                    along = b if along is None else along + b
                wallward = scale * (here * d_v + d_vv) + fix[1]
                buf[1, z, at, :] = across * metric + along + wallward

    def send(g):
        planes = pl.ds(g * GROUP, GROUP)
        return pltpu.make_async_copy(buf.at[:, planes], out.at[:, planes], sems.at[g])

    def step(g, _=None, ahead=3):
        complete(g)
        send(g).start()
        if ahead > 0:
            make_slopes()
            make_turned(g + 1)
        if ahead > 1:
            make_halves(g + 2)
        if ahead > 2:
            make_v(g + 3)
        return 0

    for g in range(groups - 4):
        step(g)
    for g, ahead in ((groups - 4, 2), (groups - 3, 2), (groups - 2, 1), (groups - 1, 0)):
        step(g, ahead=ahead)
    for g in range(groups):
        send(g).wait()


def call(body, name, inputs, outputs, scratch, flops, moved, limit, far=(), aliases=None):
    return pl.pallas_call(
        body,
        name=name,
        in_specs=[HBM if i in far else WHOLE for i in range(len(inputs))],
        out_specs=tuple(HBM if isinstance(o, jax.ShapeDtypeStruct) else WHOLE for o in outputs),
        out_shape=tuple(outputs),
        scratch_shapes=scratch,
        input_output_aliases=aliases or {},
        cost_estimate=pl.CostEstimate(flops=flops, bytes_accessed=moved, transcendentals=0),
        compiler_params=pltpu.CompilerParams(vmem_limit_bytes=limit),
    )(*inputs)


def keep(*values):
    return [pltpu.with_memory_space_constraint(value, pltpu.VMEM) for value in values]


def shards(velocity, stream_metric, wall_metric):
    _, nz, columns, rows_here = velocity.shape
    n_gy = lax.axis_size("gy")
    last = n_gy - 1
    padded = columns + 2 * EDGE
    rows = columns + EDGE
    metric = stream_metric.reshape(2, columns)
    wall = wall_metric.reshape(n_gy, rows_here)
    volume = nz * columns * rows_here
    mib = 1 << 20
    vmem = lambda *shape: pltpu.VMEM(shape, F32)
    pad_shape = vmem(2, nz, padded, LANES)
    token_shape = vmem(rows, LANES)

    sent = jnp.concatenate([velocity[:, :, :EDGE], velocity[:, :, columns - EDGE :]], axis=2)
    xr = lax.ppermute(sent, "gx", [(0, 1), (1, 0)])

    near = pltpu.with_memory_space_constraint(velocity, pltpu.HBM)
    metric = pltpu.with_memory_space_constraint(metric, pltpu.HBM)
    wall = pltpu.with_memory_space_constraint(wall, pltpu.HBM)
    pad, uw, ms, mh, vectors, matrix, bits, masks = call(
        lambda *refs: sum_rows(nz, last, *refs),
        "sum_rows",
        (near, metric, wall),
        [pad_shape, vmem(columns, LANES), vmem(padded, LANES), vmem(padded, LANES), vmem(8, LANES), pltpu.VMEM((2 * LANES, LANES), BF16), vmem(8, LANES), pltpu.VMEM((8 * nz, 2 * LANES), BF16)],
        [vmem(2, columns), vmem(n_gy, rows_here), pltpu.SemaphoreType.DMA((6,))],
        4 * volume,
        8 * volume,
        2 * mib,
        far=(0, 1, 2),
    )
    pad, uw, ms, mh, vectors, matrix, masks = keep(pad, uw, ms, mh, vectors, matrix, masks)
    (sums,) = call(
        lambda *refs: sum_slopes(nz, *refs),
        "sum_slopes",
        (xr, uw, ms, vectors),
        [vmem(rows, LANES)],
        [vmem(padded, LANES)],
        volume // 4,
        volume // 2,
        2 * mib,
    )

    def scan_step(level, total, below, token=None):
        came = lax.ppermute(total, "gy", [(i, i ^ (1 << level)) for i in range(n_gy)])
        below = below + came * bits[level : level + 1]
        total = total + came
        return (total if token is None else total + token), below, came

    half = lambda count: pltpu.VMEM((count, 2 * LANES), BF16)
    groups = nz // GROUP
    blocks = columns // 8
    first_groups, first_blocks = groups // 2, blocks // 2
    half = lambda count: pltpu.VMEM((count, 2 * LANES), BF16)
    prepared = [vmem(nz, padded, LANES), vmem(2, nz, columns, LANES), vmem(9 * nz, LANES), vmem(9 * nz, LANES), token_shape]
    prepare_scratch = [half(2 * LANES)] * 3 + [
        half(GROUP * rows),
        half(GROUP * columns),
        half(GROUP * columns),
        vmem(GROUP, rows, LANES),
        vmem(GROUP, 24, LANES),
    ]
    pad, v0, dwall, strip_a, strip_b, token = call(
        lambda *refs: prepare_first(nz, 0, first_groups, *refs),
        "prepare_first",
        (pad, xr, ms, vectors, matrix),
        [pad_shape] + prepared,
        prepare_scratch,
        30 * volume,
        4 * volume,
        6 * mib,
        aliases={0: 0},
    )
    pad, v0, dwall, strip_a, strip_b = keep(pad, v0, dwall, strip_a, strip_b)
    total, below, came = scan_step(0, sums, jnp.zeros_like(sums), token)
    v0, dwall, strip_a, strip_b, token = call(
        lambda *refs: prepare_last(nz, first_groups, groups - first_groups, *refs),
        "prepare_last",
        (pad, v0, dwall, strip_a, strip_b, ms, vectors, matrix, came),
        prepared,
        prepare_scratch,
        30 * volume,
        4 * volume,
        6 * mib,
        aliases={1: 0, 2: 1, 3: 2, 4: 3},
    )
    v0, dwall = keep(v0, dwall)
    total, below, came = scan_step(1, total, below, token)

    got_a = lax.ppermute(strip_a, "gy", [(i, i ^ 1) for i in range(n_gy)])
    got_b = lax.ppermute(strip_b, "gy", [(i, i + 1) if i % 2 else (i, i - 1) for i in range(1, last)])
    known = [vmem(2, nz, columns, LANES), vmem(3, nz, padded, LANES), vmem(3, nz, columns, LANES), token_shape]
    part, gxs, gzs, token = call(
        lambda *refs: known_first(nz, first_blocks, *refs),
        "known_first",
        (pad, mh, came),
        known,
        [],
        40 * volume,
        4 * volume,
        4 * mib,
    )
    part, gxs, gzs = keep(part, gxs, gzs)
    total, below, came = scan_step(2, total, below, token)
    part, gxs, gzs, token = call(
        lambda *refs: known_last(nz, first_blocks, *refs),
        "known_last",
        (pad, part, gxs, gzs, mh, came, got_a, came),
        known,
        [],
        40 * volume,
        4 * volume,
        4 * mib,
        aliases={1: 0, 2: 1, 3: 2},
    )
    part, gxs, gzs = keep(part, gxs, gzs)

    level = 3
    while (1 << level) < n_gy:
        total, below, came = scan_step(level, total, below)
        level += 1

    (out,) = call(
        lambda *refs: finish(nz, last, *refs),
        "finish",
        (pad, v0, part, dwall, gxs, gzs, mh, vectors, matrix, masks, strip_a, strip_b, got_a, got_b, below, total, sums),
        [jax.ShapeDtypeStruct((3, nz, columns, rows_here), F32)],
        [
            vmem(nz, padded, LANES),
            vmem(3, nz, columns, LANES),
            vmem(24 * nz, LANES),
            half(2 * rows),
            half(4 * GROUP * columns),
            vmem(4 * GROUP * columns, LANES),
            vmem(GROUP, columns, LANES),
            pltpu.SemaphoreType.DMA((nz // GROUP,)),
        ],
        80 * volume,
        20 * volume,
        16 * mib,
    )
    return out


def solution(mesh):
    in_specs = (P(None, None, "gx", "gy"), P(), P())
    out_specs = P(None, None, "gx", "gy")
    return jax.shard_map(shards, mesh=mesh, in_specs=in_specs, out_specs=out_specs, check_vma=False)
```

```python
import jax
import jax.numpy as jnp
from jax import lax
from jax.experimental import pallas as pl
from jax.experimental.pallas import tpu as pltpu
from jax.sharding import PartitionSpec as P

F32 = jnp.float32
BF16 = jnp.bfloat16
HALF60 = 0.5 / 60.0
CENTRAL = ((1, 45.0), (2, -9.0), (3, 1.0))
WALL_ROWS = (
    {0: -110.0, 1: 180.0, 2: -90.0, 3: 20.0},
    {-1: -20.0, 0: -30.0, 1: 60.0, 2: -10.0},
    {-2: 5.0, -1: -40.0, 1: 40.0, 2: -5.0},
)
LANES = 128
GROUP = 4
EDGE = 8
LOW = EDGE - 3

WHOLE = pl.BlockSpec(memory_space=pltpu.VMEM)
HBM = pl.BlockSpec(memory_space=pltpu.HBM)


def iota(shape, dim):
    return lax.broadcasted_iota(jnp.int32, shape, dim)


def split(value):
    high = value.astype(BF16)
    low = (value - high.astype(F32)).astype(BF16)
    return jnp.concatenate([high, low], axis=1)


def wrapped(plane, nz):
    return lax.rem(plane + nz, nz)


def wall_matrix(place, last):
    h = iota((LANES, LANES), 0)
    j = iota((LANES, LANES), 1)
    away = h - j
    inner = jnp.zeros((LANES, LANES), F32)
    for distance, weight in CENTRAL:
        inner = jnp.where(away == distance, weight, inner)
        inner = jnp.where(away == -distance, -weight, inner)
    for row, entries in enumerate(WALL_ROWS):
        for side in (0, 1):
            at = row if side == 0 else LANES - 1 - row
            sign = 1 if side == 0 else -1
            closed = jnp.zeros((LANES, LANES), F32)
            for offset, weight in entries.items():
                closed = jnp.where(away == sign * offset, sign * weight, closed)
            here = jnp.where(place == (0 if side == 0 else last), 1, 0)
            inner = jnp.where((j == at) & (here == 1), closed, inner)
    inner = inner.astype(BF16)
    return jnp.concatenate([inner, inner], axis=0)


def heights(wall, block, blocks):
    cell = 1.0 / wall[...]
    row = iota(cell.shape, 0)
    total = jnp.sum(cell)
    before = jnp.sum(jnp.where(row < block, cell, 0.0))
    mine = 1.0 / wall[pl.ds(block, 1), :]
    prefix = mine
    lane = iota((1, LANES), 1)
    for shift in (1, 2, 4, 8, 16, 32, 64):
        prefix = prefix + jnp.where(lane >= shift, pltpu.roll(prefix, shift, 1), 0.0)
    return (before + prefix - 0.5 * mine) / total


def sum_rows(nz, last, vel, metric_hbm, wall_hbm, pad, uw, ms, mh, vectors, matrix, bits, masks, metric, wall, sems):
    gx = lax.axis_index("gx")
    gy = lax.axis_index("gy")
    columns = uw.shape[0]
    chunks = 4
    per = nz // chunks

    def chunk(c):
        planes = pl.ds(c * per, per)
        return pltpu.make_async_copy(vel.at[:, planes], pad.at[:, planes, pl.ds(EDGE, columns)], sems.at[c])

    small = [
        pltpu.make_async_copy(wall_hbm, wall, sems.at[chunks]),
        pltpu.make_async_copy(metric_hbm, metric, sems.at[chunks + 1]),
    ]
    for copy in small:
        copy.start()
    for c in range(chunks):
        chunk(c).start()
    matrix[...] = wall_matrix(gy, last)
    plane = iota(masks.shape, 0) // 8
    masks[...] = jnp.where(lax.rem(iota(masks.shape, 1), nz) == plane, 1.0, 0.0).astype(BF16)
    for copy in small:
        copy.wait()
    own = jnp.broadcast_to(metric[pl.ds(gx, 1), :], (LANES, columns)).T
    peer = jnp.broadcast_to(metric[pl.ds(1 - gx, 1), :], (LANES, columns)).T
    ms[0:EDGE, :] = peer[columns - EDGE :]
    ms[EDGE : EDGE + columns, :] = own
    ms[EDGE + columns :, :] = peer[:EDGE]
    mh[...] = ms[...] * HALF60
    wall_here = wall[pl.ds(gy, 1), :]
    rw = 1.0 / wall_here
    vectors[0:1, :] = heights(wall, jnp.maximum(gy - 1, 0), last + 1)
    vectors[1:2, :] = heights(wall, gy, last + 1)
    vectors[2:3, :] = heights(wall, jnp.minimum(gy + 1, last), last + 1)
    vectors[3:4, :] = wall_here * HALF60
    vectors[4:5, :] = rw
    vectors[5:8, :] = jnp.zeros((3, LANES), F32)
    for i in range(bits.shape[0]):
        bits[i : i + 1, :] = jnp.full((1, LANES), jnp.where((gy & (1 << i)) != 0, 1.0, 0.0), F32)
    lane = iota((columns, LANES), 1)

    ones = jnp.ones((2 * LANES, LANES), BF16)

    def group(g, held):
        chunk(g).wait()
        weighted = [pad[1, g * per + p, pl.ds(EDGE, columns), :] * rw for p in range(per)]
        lines = jnp.dot(split(jnp.concatenate(weighted, axis=0)), ones, preferred_element_type=F32)
        for p in range(per):
            z = g * per + p
            line = jnp.sum(pad[0, z, pl.ds(EDGE, columns), :] * rw, axis=1, keepdims=True)
            held = jnp.where(lane == z, line, held)
            held = jnp.where(lane == z + nz, lines[p * columns : (p + 1) * columns], held)
        return held

    uw[...] = lax.fori_loop(0, chunks, group, jnp.zeros((columns, LANES), F32))


def sum_slopes(nz, xr, uw, ms, vectors, sums, wide):
    columns = uw.shape[0]
    rows = columns + EDGE
    rw = vectors[4:5, :]
    lane = iota((2 * EDGE, LANES), 1)
    held = jnp.zeros((2 * EDGE, LANES), F32)
    for z in range(nz):
        for c in range(2):
            line = jnp.sum(xr[c, z] * rw, axis=1, keepdims=True)
            held = jnp.where(lane == z + c * nz, line, held)
    wide[0:EDGE, :] = held[EDGE:]
    wide[EDGE : EDGE + columns, :] = uw[...]
    wide[EDGE + columns :, :] = held[:EDGE]
    centre = wide[pl.ds(LOW, rows), :]
    lane = iota((rows, LANES), 1)
    around = jnp.where(lane < nz, pltpu.roll(centre, LANES - nz, 1), centre)
    around = jnp.where(lane < 2 * nz, around, pltpu.roll(around, 2 * nz, 1))
    du = dw = None
    for distance, weight in CENTRAL:
        a = weight * (wide[pl.ds(LOW + distance, rows), :] - wide[pl.ds(LOW - distance, rows), :])
        b = weight * (pltpu.roll(around, LANES - distance, 1) - pltpu.roll(around, distance, 1))
        du = a if du is None else du + a
        dw = b if dw is None else dw + b
    total = (ms[pl.ds(LOW, rows), :] * du + dw) * (1.0 / 60.0)
    sums[...] = jnp.where(lane < nz, total, 0.0)


def edge_columns(first_lane):
    h = iota((LANES, LANES), 0)
    lane = iota((LANES, LANES), 1) - first_lane
    last = (lane >= 0) & (lane < 3) & (h == lane + LANES - 3)
    first = (lane >= 3) & (lane < 6) & (h == lane - 3)
    picked = jnp.where(last | first, 1.0, 0.0).astype(BF16)
    return jnp.concatenate([picked, picked], axis=0)


def prepare(
    nz, first, count, pad, ms, vectors, matrix, v0, dwall, strip_a, strip_b, token,
    weights_s, weights_u, weights_w, halves_s, halves_u, halves_w, edges, turned,
):
    gy = lax.axis_index("gy")
    columns = dwall.shape[2]
    rows = columns + EDGE
    tall = rows // 8
    rw60 = vectors[4:5, :] * (1.0 / 60.0)
    scale = vectors[3:4, :]
    h = iota((LANES, LANES), 0)
    j = iota((LANES, LANES), 1)
    climb = jnp.where(h < j, -1.0, jnp.where(h == j, -0.5, 0.0)).astype(BF16)
    weights_s[:, :LANES] = jnp.concatenate([climb, climb], axis=0)
    weights_s[:, LANES:] = edge_columns(12)
    weights_u[:, :LANES] = matrix[...]
    weights_u[:, LANES:] = edge_columns(0)
    weights_w[:, :LANES] = matrix[...]
    weights_w[:, LANES:] = edge_columns(6)
    odd = lax.rem(gy, 2) == 1
    token[...] = jnp.zeros(token.shape, F32)

    def gather(g):
        blocks = []
        for p in range(GROUP):
            z = g * GROUP + p
            ups = [wrapped(z + d, nz) for d in (1, 2, 3)]
            downs = [wrapped(z - d, nz) for d in (1, 2, 3)]
            for k in range(tall):
                r = LOW + 8 * k
                du = dw = None
                for distance, weight in CENTRAL:
                    a = pad[0, z, pl.ds(r + distance, 8), :] - pad[0, z, pl.ds(r - distance, 8), :]
                    b = pad[1, ups[distance - 1], pl.ds(r, 8), :] - pad[1, downs[distance - 1], pl.ds(r, 8), :]
                    if weight != 1.0:
                        a, b = weight * a, weight * b
                    du = a if du is None else du + a
                    dw = b if dw is None else dw + b
                blocks.append((ms[pl.ds(r, 8), :] * du + dw) * rw60)
                if len(blocks) == 2:
                    halves_s[pl.ds(8 * (p * tall + k - 1), 16), :] = split(jnp.concatenate(blocks, axis=0))
                    blocks = []
            halves_u[pl.ds(p * columns, columns), :] = split(pad[0, z, pl.ds(EDGE, columns), :])
            halves_w[pl.ds(p * columns, columns), :] = split(pad[1, z, pl.ds(EDGE, columns), :])

    def settle(g):
        made_s = jnp.dot(halves_s[...], weights_s[...], preferred_element_type=F32)
        for p in range(GROUP):
            here = made_s[p * rows : (p + 1) * rows]
            v0[g * GROUP + p, pl.ds(LOW, rows), :] = here[:, :LANES]
            edges[p] = here[:, LANES:]
        made_u = jnp.dot(halves_u[...], weights_u[...], preferred_element_type=F32)
        made_w = jnp.dot(halves_w[...], weights_w[...], preferred_element_type=F32)
        for p in range(GROUP):
            z = g * GROUP + p
            at = slice(p * columns, (p + 1) * columns)
            dwall[0, z] = made_u[at, :LANES] * scale
            dwall[1, z] = made_w[at, :LANES] * scale
            packed = made_u[at, LANES:] + made_w[at, LANES:] + edges[p, pl.ds(3, columns), :]
            turned[p] = packed.T[:24]
            for f in range(3):
                high = turned[p, 6 * f : 6 * f + 3, :]
                low = turned[p, 6 * f + 3 : 6 * f + 6, :]
                strip_a[pl.ds(3 * f * nz + z, 3, stride=nz), :] = jnp.where(odd, low, high)
                strip_b[pl.ds(3 * f * nz + z, 3, stride=nz), :] = jnp.where(odd, high, low)

    def step(g, _):
        settle(g)
        gather(g + 1)
        return 0

    gather(first)
    lax.fori_loop(first, first + count - 1, step, 0)
    settle(first + count - 1)


def prepare_first(nz, first, count, pad_in, xr, ms, vectors, matrix, pad, *rest):
    del pad_in
    columns = pad.shape[2] - 2 * EDGE
    pad[:, :, pl.ds(0, EDGE), :] = xr[:, :, pl.ds(EDGE, EDGE), :]
    pad[:, :, pl.ds(EDGE + columns, EDGE), :] = xr[:, :, pl.ds(0, EDGE), :]
    prepare(nz, first, count, pad, ms, vectors, matrix, *rest)


def prepare_last(nz, first, count, pad, v0, dwall, strip_a, strip_b, ms, vectors, matrix, wait, *rest):
    del v0, dwall, strip_a, strip_b, wait
    prepare(nz, first, count, pad, ms, vectors, matrix, *rest)


def known_first(nz, count, pad, mh, wait, part, gx_out, gz_out, token):
    del wait
    for z in range(nz):
        u = pad[0, z, pl.ds(0, 8), :]
        for distance, weight in CENTRAL:
            gx_out[distance - 1, z, pl.ds(0, 8), :] = weight * (u + pad[0, z, pl.ds(distance, 8), :])
    known_terms(nz, 0, count, pad, mh, part, gx_out, gz_out, token)


def known_last(nz, first, pad, part_in, gx_in, gz_in, mh, wait_a, wait_b, wait_c, part, gx_out, gz_out, token):
    del part_in, gx_in, gz_in, wait_a, wait_b, wait_c
    known_terms(nz, first, part.shape[2] // 8 - first, pad, mh, part, gx_out, gz_out, token)


def known_terms(nz, first, count, pad, mh, part, gx_out, gz_out, token):
    token[...] = jnp.zeros(token.shape, F32)

    def block(k, _):
        r = pl.multiple_of(8 * k + EDGE, 8)
        at = pl.ds(pl.multiple_of(8 * k, 8), 8)
        metric = mh[pl.ds(r, 8), :]
        field = [{}, {}]
        factor = {}

        def load(c, z):
            if z not in field[c]:
                field[c][z] = pad[c, z % nz, pl.ds(r, 8), :]
            return field[c][z]

        def span_factor(distance, weight, z):
            if (distance, z) not in factor:
                factor[distance, z] = (load(1, z) + load(1, z + distance)) * (weight * HALF60)
            return factor[distance, z]

        for z in range(nz):
            u = load(0, z)
            across = [None, None]
            along = [None, None]
            for distance, weight in CENTRAL:
                ahead = [pad[c, z, pl.ds(r + distance, 8), :] for c in range(2)]
                behind = [pad[c, z, pl.ds(r - distance, 8), :] for c in range(2)]
                g, g_low = u + ahead[0], u + behind[0]
                if weight != 1.0:
                    g, g_low = weight * g, weight * g_low
                gx_out[distance - 1, z, pl.ds(r, 8), :] = g
                s = span_factor(distance, weight, z)
                s_low = span_factor(distance, weight, z - distance)
                gz_out[distance - 1, z, at, :] = s
                for c in range(2):
                    a = g * ahead[c] - g_low * behind[c]
                    b = s * load(c, z + distance) - s_low * load(c, z - distance)
                    across[c] = a if across[c] is None else across[c] + a
                    along[c] = b if along[c] is None else along[c] + b
            for c in range(2):
                part[c, z, at, :] = across[c] * metric + along[c]
        return 0

    lax.fori_loop(first, first + count, block, 0)


def finish(
    nz, last, pad, v0, part, dwall, gxs, gzs, mh, vectors, matrix, masks, own_a, own_b, got_a, got_b, below, total, sums,
    out, v, buf, fixes, lhs, halves, slopes, turned, sems,
):
    gy = lax.axis_index("gy")
    columns = buf.shape[2]
    rows = columns + EDGE
    odd = lax.rem(gy, 2) == 1
    frac_low, frac, frac_high, scale = (vectors[i : i + 1, :] for i in range(4))

    def strip(pick, f, r):
        at = pl.ds((3 * f + r) * nz, nz)
        return pick[0][at, :], pick[1][at, :]

    def own_first(f, r):
        a, b = strip((own_a, own_b), f, r)
        return jnp.where(odd, a, b)

    def own_last(f, r):
        a, b = strip((own_a, own_b), f, r)
        return jnp.where(odd, b, a)

    def from_low(f, r):
        a, b = strip((got_a, got_b), f, r)
        return jnp.where(odd, a, b)

    def from_high(f, r):
        a, b = strip((got_a, got_b), f, r)
        return jnp.where(odd, b, a)

    def compact(ref):
        return ref[pl.ds(3, columns), :].T[:nz]

    below_c = compact(below)
    total_c = compact(total)
    incl_c = below_c + compact(sums)
    lane_one = lambda vector, at: vector[:, at : at + 1]

    def climb(start, slopes, sign, fractions):
        level, made = start, []
        for slope, fraction in zip(slopes, fractions):
            made.append(fraction * total_c - (level + (0.5 * sign) * slope))
            level = level + sign * slope
        return made

    v_first = climb(below_c, [own_first(2, r) for r in range(3)], 1.0, [lane_one(frac, r) for r in range(3)])
    v_last = climb(incl_c, [own_last(2, 2 - q) for q in range(3)], -1.0, [lane_one(frac, LANES - 1 - q) for q in range(3)])
    v_low = climb(below_c, [from_low(2, 2 - q) for q in range(3)], -1.0, [lane_one(frac_low, LANES - 1 - q) for q in range(3)])
    v_high = climb(incl_c, [from_high(2, r) for r in range(3)], 1.0, [lane_one(frac_high, r) for r in range(3)])
    v_low = [jnp.where(gy > 0, x, 0.0) for x in v_low]
    v_high = [jnp.where(gy < last, x, 0.0) for x in v_high]
    weight_of = dict(CENTRAL)
    for i in (15, 16, 17, 18, 19, 20):
        fixes[pl.ds(i * nz, nz), :] = jnp.zeros((nz, LANES), F32)
    for c in range(3):
        for side in range(2):
            v_own, v_out = (v_first, v_low) if side == 0 else (v_last, v_high)
            for q in range(3):
                value = None
                for m in range(3 - q):
                    if c == 1:
                        field = v_out[m]
                    elif side == 0:
                        field = from_low(c // 2, 2 - m)
                    else:
                        field = from_high(c // 2, m)
                    weight = weight_of[q + m + 1] * (-1.0 if side == 0 else 1.0)
                    term = weight * ((v_own[q] + v_out[m]) * field)
                    value = term if value is None else value + term
                at = q if side == 0 else LANES - 1 - q
                if c == 0:
                    row = q if side == 0 else 23 - q
                else:
                    row = 6 * c - 3 + (3 + q if side == 0 else 2 - q)
                fixes[pl.ds(row * nz, nz), :] = value * lane_one(scale, at)

    below_v = below[...]
    total_v = total[...]
    below_h = below_v.astype(BF16).astype(F32)
    below_l = below_v - below_h
    total_h = total_v.astype(BF16).astype(F32)
    total_l = total_v - total_h
    quarter = iota((rows, LANES), 1) // nz
    first_half = jnp.where(
        quarter == 0,
        below_h,
        jnp.where(
            quarter == 1,
            pltpu.roll(below_l, nz, 1),
            jnp.where(quarter == 2, pltpu.roll(total_h, 2 * nz, 1), pltpu.roll(total_l, 3 * nz, 1)),
        ),
    )
    second_half = jnp.where(quarter == 0, total_h, jnp.where(quarter == 1, pltpu.roll(total_l, nz, 1), 0.0))
    both = jnp.concatenate([first_half, second_half], axis=1).astype(BF16).astype(F32)
    for k in range(rows // 8):
        block = both[8 * k : 8 * k + 8]
        lhs[pl.ds(16 * k, 16), :] = jnp.concatenate([block, block], axis=0).astype(BF16)
    frac_h = frac.astype(BF16).astype(F32)
    frac_l = frac - frac_h
    k_index = iota((2 * LANES, LANES), 0)
    base = jnp.where(
        k_index < 2 * nz,
        -1.0,
        jnp.where(k_index < LANES, jnp.broadcast_to(frac_h, (2 * LANES, LANES)), jnp.broadcast_to(frac_l, (2 * LANES, LANES))),
    ).astype(BF16)
    tall = rows // 8

    def make_v(g):
        chosen = []
        for pair in range(GROUP // 2):
            mask = masks[pl.ds(pl.multiple_of(8 * (g * GROUP + 2 * pair), 16), 16), :]
            chosen += [lhs[pl.ds(16 * k, 16), :] * mask for k in range(tall)]
        level = jnp.dot(jnp.concatenate(chosen, axis=0), base, preferred_element_type=F32)
        for p in range(GROUP):
            for k in range(tall):
                at = pl.ds(LOW + 8 * k, 8)
                row = 16 * (p // 2 * tall + k) + 8 * (p % 2)
                v[g * GROUP + p, at, :] = v0[g * GROUP + p, at, :] + level[row : row + 8]

    def make_halves(g):
        for p in range(GROUP):
            z = g * GROUP + p
            here = v[z, pl.ds(EDGE, columns), :]
            for i, factor in enumerate((None, here, pad[0, z, pl.ds(EDGE, columns), :], pad[1, z, pl.ds(EDGE, columns), :])):
                halves[pl.ds((4 * p + i) * columns, columns), :] = split(here if factor is None else here * factor)

    def make_slopes():
        slopes[...] = jnp.dot(halves[...], matrix[...], preferred_element_type=F32)

    zeros = jnp.zeros((LANES - 24, LANES), F32)

    def make_turned(g):
        for p in range(GROUP):
            z = g * GROUP + p
            low = fixes[pl.ds(z, 16, stride=nz), :]
            high = fixes[pl.ds(16 * nz + z, 8, stride=nz), :]
            turned[p] = jnp.concatenate([low, zeros, high], axis=0).T

    groups = nz // GROUP
    for g in (groups - 1, 0, 1, 2):
        make_v(g)
    make_halves(0)
    make_slopes()
    make_turned(0)
    make_halves(1)
    lane = iota((8, LANES), 1)
    at_edge = (lane < 3) | (lane >= LANES - 3)

    def complete(g):
        for k in range(columns // 8):
            r = EDGE + 8 * k
            at = pl.ds(8 * k, 8)
            metric = mh[pl.ds(r, 8), :]
            level, factor = {}, {}

            def v_at(g, p):
                if p not in level:
                    level[p] = v[wrapped(g * GROUP + p, nz), pl.ds(r, 8), :]
                return level[p]

            def span_factor(g, distance, p):
                if (distance, p) not in factor:
                    factor[distance, p] = gzs[distance - 1, wrapped(g * GROUP + p, nz), at, :]
                return factor[distance, p]

            for p in range(GROUP):
                z = g * GROUP + p
                here = v_at(g, p)
                edge = turned[p, at, :]
                fix = [edge, pltpu.roll(edge, LANES - 6, 1), pltpu.roll(edge, LANES - 12, 1)]
                fix = [jnp.where(at_edge, x, 0.0) for x in fix]
                d_v, d_vv, d_vu, d_vw = (slopes[pl.ds((4 * p + i) * columns + 8 * k, 8), :] for i in range(4))
                buf[0, z, at, :] = part[0, z, at, :] + here * dwall[0, z, at, :] + (scale * d_vu + fix[0])
                buf[2, z, at, :] = part[1, z, at, :] + here * dwall[1, z, at, :] + (scale * d_vw + fix[2])
                across = along = None
                for distance, _w in CENTRAL:
                    a = gxs[distance - 1, z, pl.ds(r, 8), :] * v[z, pl.ds(r + distance, 8), :]
                    a = a - gxs[distance - 1, z, pl.ds(r - distance, 8), :] * v[z, pl.ds(r - distance, 8), :]
                    b = span_factor(g, distance, p) * v_at(g, p + distance)
                    b = b - span_factor(g, distance, p - distance) * v_at(g, p - distance)
                    across = a if across is None else across + a
                    along = b if along is None else along + b
                wallward = scale * (here * d_v + d_vv) + fix[1]
                buf[1, z, at, :] = across * metric + along + wallward

    def send(g):
        planes = pl.ds(g * GROUP, GROUP)
        return pltpu.make_async_copy(buf.at[:, planes], out.at[:, planes], sems.at[g])

    def step(g, _=None, ahead=3):
        complete(g)
        send(g).start()
        if ahead > 0:
            make_slopes()
            make_turned(g + 1)
        if ahead > 1:
            make_halves(g + 2)
        if ahead > 2:
            make_v(g + 3)
        return 0

    for g in range(groups - 4):
        step(g)
    for g, ahead in ((groups - 4, 2), (groups - 3, 2), (groups - 2, 1), (groups - 1, 0)):
        step(g, ahead=ahead)
    for g in range(groups):
        send(g).wait()


def call(body, name, inputs, outputs, scratch, flops, moved, limit, far=(), aliases=None):
    return pl.pallas_call(
        body,
        name=name,
        in_specs=[HBM if i in far else WHOLE for i in range(len(inputs))],
        out_specs=tuple(HBM if isinstance(o, jax.ShapeDtypeStruct) else WHOLE for o in outputs),
        out_shape=tuple(outputs),
        scratch_shapes=scratch,
        input_output_aliases=aliases or {},
        cost_estimate=pl.CostEstimate(flops=flops, bytes_accessed=moved, transcendentals=0),
        compiler_params=pltpu.CompilerParams(vmem_limit_bytes=limit),
    )(*inputs)


def keep(*values):
    return [pltpu.with_memory_space_constraint(value, pltpu.VMEM) for value in values]


def shards(velocity, stream_metric, wall_metric):
    _, nz, columns, rows_here = velocity.shape
    n_gy = lax.axis_size("gy")
    last = n_gy - 1
    padded = columns + 2 * EDGE
    rows = columns + EDGE
    metric = stream_metric.reshape(2, columns)
    wall = wall_metric.reshape(n_gy, rows_here)
    volume = nz * columns * rows_here
    mib = 1 << 20
    vmem = lambda *shape: pltpu.VMEM(shape, F32)
    pad_shape = vmem(2, nz, padded, LANES)
    token_shape = vmem(rows, LANES)

    sent = jnp.concatenate([velocity[:, :, :EDGE], velocity[:, :, columns - EDGE :]], axis=2)
    xr = lax.ppermute(sent, "gx", [(0, 1), (1, 0)])

    near = pltpu.with_memory_space_constraint(velocity, pltpu.HBM)
    metric = pltpu.with_memory_space_constraint(metric, pltpu.HBM)
    wall = pltpu.with_memory_space_constraint(wall, pltpu.HBM)
    pad, uw, ms, mh, vectors, matrix, bits, masks = call(
        lambda *refs: sum_rows(nz, last, *refs),
        "sum_rows",
        (near, metric, wall),
        [pad_shape, vmem(columns, LANES), vmem(padded, LANES), vmem(padded, LANES), vmem(8, LANES), pltpu.VMEM((2 * LANES, LANES), BF16), vmem(8, LANES), pltpu.VMEM((8 * nz, 2 * LANES), BF16)],
        [vmem(2, columns), vmem(n_gy, rows_here), pltpu.SemaphoreType.DMA((6,))],
        4 * volume,
        8 * volume,
        2 * mib,
        far=(0, 1, 2),
    )
    pad, uw, ms, mh, vectors, matrix, masks = keep(pad, uw, ms, mh, vectors, matrix, masks)
    (sums,) = call(
        lambda *refs: sum_slopes(nz, *refs),
        "sum_slopes",
        (xr, uw, ms, vectors),
        [vmem(rows, LANES)],
        [vmem(padded, LANES)],
        volume // 4,
        volume // 2,
        2 * mib,
    )

    def scan_step(level, total, below, token=None):
        came = lax.ppermute(total, "gy", [(i, i ^ (1 << level)) for i in range(n_gy)])
        below = below + came * bits[level : level + 1]
        total = total + came
        return (total if token is None else total + token), below, came

    half = lambda count: pltpu.VMEM((count, 2 * LANES), BF16)
    groups = nz // GROUP
    blocks = columns // 8
    first_groups, first_blocks = groups // 2, blocks // 2
    half = lambda count: pltpu.VMEM((count, 2 * LANES), BF16)
    prepared = [vmem(nz, padded, LANES), vmem(2, nz, columns, LANES), vmem(9 * nz, LANES), vmem(9 * nz, LANES), token_shape]
    prepare_scratch = [half(2 * LANES)] * 3 + [
        half(GROUP * rows),
        half(GROUP * columns),
        half(GROUP * columns),
        vmem(GROUP, rows, LANES),
        vmem(GROUP, 24, LANES),
    ]
    pad, v0, dwall, strip_a, strip_b, token = call(
        lambda *refs: prepare_first(nz, 0, first_groups, *refs),
        "prepare_first",
        (pad, xr, ms, vectors, matrix),
        [pad_shape] + prepared,
        prepare_scratch,
        30 * volume,
        4 * volume,
        6 * mib,
        aliases={0: 0},
    )
    pad, v0, dwall, strip_a, strip_b = keep(pad, v0, dwall, strip_a, strip_b)
    total, below, came = scan_step(0, sums, jnp.zeros_like(sums), token)
    v0, dwall, strip_a, strip_b, token = call(
        lambda *refs: prepare_last(nz, first_groups, groups - first_groups, *refs),
        "prepare_last",
        (pad, v0, dwall, strip_a, strip_b, ms, vectors, matrix, came),
        prepared,
        prepare_scratch,
        30 * volume,
        4 * volume,
        6 * mib,
        aliases={1: 0, 2: 1, 3: 2, 4: 3},
    )
    v0, dwall = keep(v0, dwall)
    total, below, came = scan_step(1, total, below, token)

    got_a = lax.ppermute(strip_a, "gy", [(i, i ^ 1) for i in range(n_gy)])
    got_b = lax.ppermute(strip_b, "gy", [(i, i + 1) if i % 2 else (i, i - 1) for i in range(1, last)])
    known = [vmem(2, nz, columns, LANES), vmem(3, nz, padded, LANES), vmem(3, nz, columns, LANES), token_shape]
    part, gxs, gzs, token = call(
        lambda *refs: known_first(nz, first_blocks, *refs),
        "known_first",
        (pad, mh, came),
        known,
        [],
        40 * volume,
        4 * volume,
        4 * mib,
    )
    part, gxs, gzs = keep(part, gxs, gzs)
    total, below, came = scan_step(2, total, below, token)
    part, gxs, gzs, token = call(
        lambda *refs: known_last(nz, first_blocks, *refs),
        "known_last",
        (pad, part, gxs, gzs, mh, came, got_a, came),
        known,
        [],
        40 * volume,
        4 * volume,
        4 * mib,
        aliases={1: 0, 2: 1, 3: 2},
    )
    part, gxs, gzs = keep(part, gxs, gzs)

    level = 3
    while (1 << level) < n_gy:
        total, below, came = scan_step(level, total, below)
        level += 1

    (out,) = call(
        lambda *refs: finish(nz, last, *refs),
        "finish",
        (pad, v0, part, dwall, gxs, gzs, mh, vectors, matrix, masks, strip_a, strip_b, got_a, got_b, below, total, sums),
        [jax.ShapeDtypeStruct((3, nz, columns, rows_here), F32)],
        [
            vmem(nz, padded, LANES),
            vmem(3, nz, columns, LANES),
            vmem(24 * nz, LANES),
            half(2 * rows),
            half(4 * GROUP * columns),
            vmem(4 * GROUP * columns, LANES),
            vmem(GROUP, columns, LANES),
            pltpu.SemaphoreType.DMA((nz // GROUP,)),
        ],
        80 * volume,
        20 * volume,
        16 * mib,
    )
    return out


def solution(mesh):
    in_specs = (P(None, None, "gx", "gy"), P(), P())
    out_specs = P(None, None, "gx", "gy")
    return jax.shard_map(shards, mesh=mesh, in_specs=in_specs, out_specs=out_specs, check_vma=False)
```
